128 devices in a mesh: dp: 4 (over z_hi, core), seq: 32 (over x, z_lo, y).
Axes of the slice: x: 4, y: 4, z: 4 (z_hi: 2, z_lo: 2; z = z_hi * 2 + z_lo), core: 2. Of those that a mesh axis runs over, the one named last changes fastest.
Arguments:
- block_input: bfloat16 [4, 32, 256, 1152], P('dp', 'seq'), may hold values from -45 to 45
- out_grad: bfloat16 [4, 32, 256, 1152], P('dp', 'seq'), may hold values from -6 to 6
- spatial_keep: int32 [4, 32, 256, 1152], P('dp', 'seq'), may hold values 0 or 1
- temporal_keep: int32 [4, 32, 256, 1152], P('dp', None, 'seq'), may hold values 0 or 1
- spatial_qkv: bfloat16 [1152, 1728], replicated, may hold values from -0.1875 to 0.1875
- spatial_out: bfloat16 [1152, 576], replicated, may hold values from -0.25 to 0.25
- temporal_qkv: bfloat16 [1152, 1728], replicated, may hold values from -0.1875 to 0.1875
- temporal_out: bfloat16 [1152, 576], replicated, may hold values from -0.25 to 0.25
Outputs:
- input_grad: bfloat16 [4, 32, 256, 1152], P('dp', 'seq')
- spatial_qkv_grad: float32 [1152, 1728], P('seq', 'dp')
- spatial_out_grad: float32 [1152, 576], P('seq', 'dp')
- temporal_qkv_grad: float32 [1152, 1728], P('seq', 'dp')
- temporal_out_grad: float32 [1152, 576], P('seq', 'dp')
The draws below stay inside these ranges and needn't reach their ends.
All inputs are finite; a program needn't handle non-finite values. No bound on the sum of `spatial_keep` or of `temporal_keep` on one device may be relied on, other than what follows from the above.
Results may differ from the reference program's by a relative error of at most 0.03.
Values may be sent and summed in bfloat16 or wider, within the bound.
A program may use at most 128 MiB of HBM per device.

```python
import math
import jax
import jax.numpy as jnp
from jax import lax

D = 1152
H = 8
HD = 72
FRAMES = 32
POS = 256
CLIPS = 4


def draw_block_input(key, part):
    key = jax.random.fold_in(key, 11)
    base_key, row_key, col_key = jax.random.split(key, 3)
    shape = (CLIPS, FRAMES, POS, D)
    base = jax.random.normal(base_key, shape, jnp.float32)
    rows = jnp.exp(jax.random.uniform(row_key, (CLIPS, FRAMES, POS, 1), jnp.float32, 0.0, math.log(10.0))) * 0.3
    base = jnp.clip(base, -5.0, 5.0)
    cols = jnp.exp(jax.random.uniform(col_key, (D,), jnp.float32, 0.0, math.log(10.0))) * 0.3
    return (base * rows * cols).astype(jnp.bfloat16)


def place_ends(result, own_key, least, high):
    shape = result.shape
    spot = [jax.random.randint(jax.random.fold_in(own_key, axis), (), 0, shape[axis]) for axis in range(len(shape))]
    result = result.at[tuple(spot)].set(least)
    longest = shape.index(max(shape))
    spot[longest] = (spot[longest] + 1) % shape[longest]
    return result.at[tuple(spot)].set(high)


def shard_levels(stream_key, shape, shards, least, top_value):
    level = 1.0
    for axis_at, shards_of in shards:
        heights = jax.random.uniform(jax.random.fold_in(jax.random.fold_in(stream_key, 6), axis_at), (shards_of,), jnp.float32, least / len(shards), top_value / len(shards))
        level = level * jnp.repeat(jnp.exp(heights), shape[axis_at] // shards_of).reshape((-1,) + (1,) * (len(shape) - 1 - axis_at))
    return level


def centred(key, shape, scale, limit, cuts=(), held_as=jnp.bfloat16):
    level = shard_levels(key, shape, cuts, -0.22, 0.18) if cuts else 1.0
    entries = jax.random.normal(key, shape, jnp.float32) * scale * level
    return jnp.minimum(jnp.maximum(entries, -limit), limit).astype(held_as)


def setup_inputs(seed: int = 0) -> dict:
    key_list = jax.random.split(jax.random.key(seed), 9)
    return {
        "block_input": draw_block_input(jax.random.fold_in(key_list[8], 71), 0),
        "out_grad": centred(key_list[1], (CLIPS, FRAMES, POS, D), 1.0, 6.0, ((0, 4), (1, 32))),
        "spatial_keep": place_ends((jax.random.randint(key_list[2], (CLIPS, FRAMES, POS, D), 0, 10) < 9).astype(jnp.int32), jax.random.fold_in(key_list[2], 1), 0, 1),
        "temporal_keep": place_ends((jax.random.randint(key_list[3], (CLIPS, FRAMES, POS, D), 0, 10) < 9).astype(jnp.int32), jax.random.fold_in(key_list[3], 1), 0, 1),
        "spatial_qkv": centred(key_list[4], (D, 3 * H * HD), D ** -0.5, 0.1875),
        "spatial_out": centred(key_list[5], (D, H * HD), (H * HD) ** -0.5, 0.25),
        "temporal_qkv": centred(key_list[6], (D, 3 * H * HD), D ** -0.5, 0.1875),
        "temporal_out": centred(key_list[7], (D, H * HD), (H * HD) ** -0.5, 0.25),
    }


def section_forward(z, w_qkv, w_out, keep):
    groups, length, extra, width = z.shape
    inner = w_out.shape[1]
    scale = HD ** (-0.5)
    zf = z.astype(jnp.float32)
    inv = lax.rsqrt(lax.optimization_barrier(jnp.mean(zf * zf, axis=-1, keepdims=True)) + 1e-06)
    normed = (zf * inv).astype(jnp.bfloat16)
    qkv = jnp.dot(normed.reshape(-1, width), w_qkv, preferred_element_type=jnp.float32).astype(jnp.bfloat16)
    qkv = qkv.reshape(groups, length, extra, 3, H, HD)
    query = qkv[:, :, :, 0]
    keys = qkv[:, :, :, 1]
    values = qkv[:, :, :, 2]
    scores = jnp.einsum('aiehc,ajehc->aehij', query.astype(jnp.float32), keys.astype(jnp.float32)) * scale
    expo = jnp.exp(scores)
    probs = expo / lax.optimization_barrier(jnp.sum(expo, axis=-1, keepdims=True))
    probs_low = probs.astype(jnp.bfloat16)
    mixed = jnp.einsum('aehij,ajehc->aiehc', probs_low.astype(jnp.float32), values.astype(jnp.float32))
    mixed = mixed.astype(jnp.bfloat16).reshape(-1, inner)
    proj = jnp.dot(mixed, w_out.T, preferred_element_type=jnp.float32).reshape(groups, length, extra, width)
    keepf = keep.astype(jnp.float32) / 0.9
    output = (zf + proj * keepf).astype(jnp.bfloat16)
    return (output, (zf, inv, normed, query, keys, values, probs, probs_low, mixed, keepf))

def section_backward(grad, saved, w_qkv, w_out):
    zf, inv, normed, query, keys, values, probs, probs_low, mixed, keepf = saved
    groups, length, extra, width = zf.shape
    inner = w_out.shape[1]
    scale = HD ** (-0.5)
    dyf = grad.astype(jnp.float32)
    d_proj = (dyf * keepf).astype(jnp.bfloat16).reshape(-1, width)
    g_out = jnp.dot(d_proj.T, mixed, preferred_element_type=jnp.float32)
    d_mixed = jnp.dot(d_proj, w_out, preferred_element_type=jnp.float32).astype(jnp.bfloat16)
    d_mixed = d_mixed.reshape(groups, length, extra, H, HD).astype(jnp.float32)
    d_probs = jnp.einsum('aiehc,ajehc->aehij', d_mixed, values.astype(jnp.float32))
    d_scores = probs * (d_probs - lax.optimization_barrier(jnp.sum(probs * d_probs, axis=-1, keepdims=True))) * scale
    d_scores = d_scores.astype(jnp.bfloat16).astype(jnp.float32)
    d_query = jnp.einsum('aehij,ajehc->aiehc', d_scores, keys.astype(jnp.float32))
    d_keys = jnp.einsum('aehij,aiehc->ajehc', d_scores, query.astype(jnp.float32))
    d_values = jnp.einsum('aehij,aiehc->ajehc', probs_low.astype(jnp.float32), d_mixed)
    d_qkv = jnp.stack([d_query, d_keys, d_values], axis=3).astype(jnp.bfloat16).reshape(-1, 3 * inner)
    g_qkv = jnp.dot(normed.reshape(-1, width).T, d_qkv, preferred_element_type=jnp.float32)
    d_normed = jnp.dot(d_qkv, w_qkv.T, preferred_element_type=jnp.float32).reshape(groups, length, extra, width)
    centered = zf * inv
    d_input = dyf + inv * (d_normed - centered * lax.optimization_barrier(jnp.mean(d_normed * centered, axis=-1, keepdims=True)))
    return (d_input, g_qkv, g_out)

def reference(block_input, out_grad, spatial_keep, temporal_keep, spatial_qkv, spatial_out, temporal_qkv, temporal_out):

    def one_clip(operands):
        clip, grad, keep_space, keep_time = operands
        first, saved_space = section_forward(clip[:, :, None, :], spatial_qkv, spatial_out, keep_space[:, :, None, :])
        first = first[:, :, 0, :]
        unused, saved_time = section_forward(first[None], temporal_qkv, temporal_out, keep_time[None])
        d_first, g_qkv_time, g_out_time = section_backward(grad[None], saved_time, temporal_qkv, temporal_out)
        d_first = d_first[0].astype(jnp.bfloat16)
        d_clip, g_qkv_space, g_out_space = section_backward(d_first[:, :, None, :], saved_space, spatial_qkv, spatial_out)
        return (d_clip[:, :, 0, :].astype(jnp.bfloat16), g_qkv_space, g_out_space, g_qkv_time, g_out_time)
    input_grad, g_qkv_space, g_out_space, g_qkv_time, g_out_time = lax.map(one_clip, (block_input, out_grad, spatial_keep, temporal_keep))
    return (input_grad, lax.optimization_barrier(jnp.sum(g_qkv_space, axis=0)), lax.optimization_barrier(jnp.sum(g_out_space, axis=0)), lax.optimization_barrier(jnp.sum(g_qkv_time, axis=0)), lax.optimization_barrier(jnp.sum(g_out_time, axis=0)))
```

```python
import jax
import jax.numpy as jnp
from jax import lax
from jax.experimental import pallas as pl
from jax.experimental.pallas import tpu as pltpu
from jax.sharding import PartitionSpec as P

D = 1152
H = 8
HD = 72
INNER = 576
T = 256
NS = 32
RB = 40
MESH = pl.DeviceIdType.MESH
BF = jnp.bfloat16
F32 = jnp.float32
SCALE = HD ** (-0.5)
KEEP = 1.0 / 0.9


def nt(a, b):
    return lax.dot_general(a, b, (((1,), (1,)), ((), ())), preferred_element_type=F32)


def tn(a, b):
    return lax.dot_general(a, b, (((0,), (0,)), ((), ())), preferred_element_type=F32)


def nn(a, b):
    return jnp.dot(a, b, preferred_element_type=F32)


SCRATCH = dict(
    x=((32, 8, D), BF),
    ks=((32, 8, D), jnp.int32),
    kt=((32, 8, D), jnp.int32),
    wqs=((D, 3 * INNER), BF),
    wos=((D, INNER), BF),
    wqt=((D, 3 * INNER), BF),
    wot=((D, INNER), BF),
    go=((NS, 8, D), BF),
    y_out=((NS, 8, D), BF),
    y_in=((NS, 8, D), BF),
    d_out=((NS, 8, D), BF),
    d_in=((NS, 8, D), BF),
    normed_s=((T, D), BF),
    normed_t=((T, D), BF),
    qkv=((T, 3 * INNER), BF),
    hs_s=((24, T, 128), BF),
    hs_t=((24, T, 128), BF),
    probs=((H, T, T), F32),
    mh_s=((H, T, 128), BF),
    mh_t=((H, T, 128), BF),
    mixed=((T, INNER), BF),
    dproj=((T, D), BF),
    dmix=((T, INNER), BF),
    dmh=((H, T, 128), BF),
    dh=((24, T, 128), BF),
    dqkv=((T, 3 * INNER), BF),
    dn=((T, D), F32),
    dsel=((2, 2, T, D), BF),
    dsel_in=((2, T, D), BF),
    perm=((32 * RB, D), BF),
    lt=((2, 32 * RB, T), BF),
    lt_in=((2, 2, 32 * RB, T), BF),
    grad=((2, 8, 4, RB, D), BF),
    r1=((2, 2, 2, 2, RB, D), BF),
    r2=((2, 2, 2, 4, RB, D), BF),
    hsum=((2, 2, 4, RB, D), BF),
    r3=((2, 2, 3, RB, D), BF),
    zsum=((2, 2, 2, RB, INNER), BF),
    r4=((2, 3, RB, INNER), BF),
    dx=((32, 8, D), BF),
)
SEMS = dict(
    load=(8,),
    store=(1,),
    a2a_s=(3, 31),
    a2a_r=(3, 31),
    core_s=(2, 3),
    core_r=(2, 3),
    r1_s=(2, 2, 2),
    r1_r=(2, 2, 2),
    r2_s=(2, 2, 2, 2),
    r2_r=(2, 2, 2, 2),
    r3_s=(2, 2, 3),
    r3_r=(2, 2, 3),
    r4_s=(2, 3),
    r4_r=(2, 3),
)


class Refs:
    pass


def body(*refs):
    ins, outs, rest = refs[:8], refs[8:13], refs[13:]
    m = Refs()
    for name, ref in zip(SCRATCH, rest[: len(SCRATCH)]):
        setattr(m, name, ref)
    for name, ref in zip(SEMS, rest[len(SCRATCH):]):
        setattr(m, name + "_sem", ref)
    dx_hbm, gqs, gos, gqt, got = outs

    dp = lax.axis_index("dp")
    me = lax.axis_index("seq")
    zh, core = dp // 2, lax.rem(dp, 2)
    cx, zl, cy = me // 8, lax.rem(me // 4, 2), lax.rem(me, 4)
    cz = zh * 2 + zl

    def place(x, y, z):
        return ((z // 2) * 2 + core, x * 8 + lax.rem(z, 2) * 4 + y)

    dests = (m.x, None, m.ks, m.kt, m.wqs, m.wos, m.wqt, m.wot)
    loads = [
        None if dst is None else pltpu.make_async_copy(src, dst, m.load_sem.at[i])
        for i, (src, dst) in enumerate(zip(ins, dests))
    ]
    for i in (0, 4, 2, 5, 7, 3, 6):
        loads[i].start()

    barrier = pltpu.get_barrier_semaphore()

    def greet(d, carry):
        pl.semaphore_signal(
            barrier, inc=1, device_id=(dp, lax.rem(me + d, NS)), device_id_type=MESH
        )
        return carry

    lax.fori_loop(1, NS, greet, 0)
    other_core = (zh * 2 + 1 - core, me)
    pl.semaphore_signal(barrier, inc=1, device_id=other_core, device_id_type=MESH)
    far = (1 - zh) * 2 + core
    pl.semaphore_signal(barrier, inc=1, device_id=(far, me), device_id_type=MESH)
    pl.semaphore_signal(
        barrier, inc=1, device_id=(far, cx * 8 + (1 - zl) * 4 + cy), device_id_type=MESH
    )

    def a2a_copy(k, src, dst, d):
        to = lax.rem(me + d, NS)
        return pltpu.make_async_remote_copy(
            src_ref=src.at[to],
            dst_ref=dst.at[me],
            send_sem=m.a2a_s_sem.at[k, d - 1],
            recv_sem=m.a2a_r_sem.at[k, d - 1],
            device_id=(dp, to),
            device_id_type=MESH,
        )

    def a2a_start(k, src, dst):
        def step(d, carry):
            a2a_copy(k, src, dst, d).start()
            return carry

        lax.fori_loop(1, NS, step, 0)

    def a2a_wait(k, src, dst):
        def step(d, carry):
            frm = lax.rem(me + NS - d, NS)
            pltpu.make_async_remote_copy(
                src_ref=src.at[frm],
                dst_ref=dst.at[frm],
                send_sem=m.a2a_s_sem.at[k, d - 1],
                recv_sem=m.a2a_r_sem.at[k, d - 1],
                device_id=(dp, frm),
                device_id_type=MESH,
            ).wait_recv()
            return carry

        lax.fori_loop(1, NS, step, 0)

    def a2a_drain(k, src, dst):
        def step(d, carry):
            a2a_copy(k, src, dst, d).wait_send()
            return carry

        lax.fori_loop(1, NS, step, 0)

    def rows(fn):
        def step(r, carry):
            fn(pl.ds(pl.multiple_of(r * 32, 32), 32), pl.ds(r * 4, 4))
            return carry

        lax.fori_loop(0, 8, step, 0)

    def flat(ref, blk):
        return ref[blk].astype(F32).reshape(32, D)

    def inv_of(zf):
        return lax.rsqrt(jnp.mean(zf * zf, axis=-1, keepdims=True) + 1e-06)

    def normalize(src, dst):
        def fn(r, blk):
            zf = flat(src, blk)
            dst[r, :] = (zf * inv_of(zf)).astype(BF)

        rows(fn)

    def split_heads(src, dst, n):
        for j in range(n):
            v = src[:, HD * j: HD * (j + 1)]
            dst[j] = jnp.concatenate([v, jnp.zeros((T, 128 - HD), BF)], axis=1)

    def qkv_heads(normed, w, hs):
        for lo, hi in ((0, 512), (512, 1024), (1024, 1536), (1536, 1728)):
            m.qkv[:, lo:hi] = nn(normed[...], w[:, lo:hi]).astype(BF)
        split_heads(m.qkv, hs, 24)

    def d_proj_mix(dy, keep, wo):
        def fn(r, blk):
            m.dproj[r, :] = (flat(dy, blk) * (flat(keep, blk) * KEEP)).astype(BF)

        rows(fn)
        m.dmix[...] = nn(m.dproj[...], wo[...]).astype(BF)
        split_heads(m.dmix, m.dmh, H)

    def softmax(q, k, mask):
        e = jnp.exp(nt(q, k) * SCALE)
        if mask is not None:
            e = jnp.where(mask, e, 0.0)
        return e / jnp.sum(e, axis=-1, keepdims=True)

    def attention_backward(h, p, p_low, q, k, v):
        dm = m.dmh[h]
        dp_ = nt(dm, v)
        ds = (p * (dp_ - jnp.sum(p * dp_, axis=-1, keepdims=True)) * SCALE).astype(BF)
        m.dh[h] = nn(ds, k).astype(BF)
        m.dh[h + 8] = tn(ds, q).astype(BF)
        m.dh[h + 16] = tn(p_low, dm).astype(BF)

    def gather_columns(sec, mh):
        for j in range(24):
            m.dqkv[:, HD * j: HD * (j + 1)] = m.dh[j][:, :HD]
        for c in range(2):
            for i in range(6):
                m.dsel[sec, c, :, HD * i: HD * (i + 1)] = m.dh[6 * c + i][:, :HD]
                lo = 432 + HD * i
                m.dsel[sec, c, :, lo: lo + HD] = m.dh[12 + 6 * c + i][:, :HD]
            for i, h in enumerate((2 * c, 2 * c + 1, 4 + 2 * c, 5 + 2 * c)):
                lo = 864 + HD * i
                m.dsel[sec, c, :, lo: lo + HD] = mh[h][:, :HD]

    def input_backward(src, dy, dst, wq):
        for n in range(3):
            m.dn[:, 384 * n: 384 * (n + 1)] = nt(m.dqkv[...], wq[384 * n: 384 * (n + 1), :])

        def fn(r, blk):
            zf = flat(src, blk)
            inv = inv_of(zf)
            c = zf * inv
            dn = m.dn[r, :]
            dz = flat(dy, blk) + inv * (dn - c * jnp.mean(dn * c, axis=-1, keepdims=True))
            dst[blk] = dz.reshape(4, 8, D).astype(BF)

        rows(fn)

    def core_copies(sec):
        pairs = (
            (m.lt.at[0], m.lt_in.at[sec, 0]),
            (m.lt.at[1], m.lt_in.at[sec, 1]),
            (m.dsel.at[sec, 1 - core], m.dsel_in.at[sec]),
        )
        return [
            pltpu.make_async_remote_copy(
                src_ref=src,
                dst_ref=dst,
                send_sem=m.core_s_sem.at[sec, i],
                recv_sem=m.core_r_sem.at[sec, i],
                device_id=other_core,
                device_id_type=MESH,
            )
            for i, (src, dst) in enumerate(pairs)
        ]

    def transpose_rows(i, src):
        def step(n, carry):
            r = pl.ds(pl.multiple_of(n * 320, 320), 320)
            m.lt[i, r, :] = nt(m.perm[r, :], src[...]).astype(BF)
            return carry

        lax.fori_loop(0, 4, step, 0)

    def weight_grads(sec):
        def step(n, carry):
            r = pl.ds(pl.multiple_of(n * 320, 320), 320)
            for i, lo, hi in ((0, 0, 384), (0, 384, 864), (1, 864, 1152)):
                acc = nn(m.lt[i, r, :], m.dsel[sec, core, :, lo:hi])
                acc = acc + nn(m.lt_in[sec, i, r, :], m.dsel_in[sec, :, lo:hi])
                m.grad[sec, pl.ds(n * 2, 2), :, :, lo:hi] = acc.reshape(
                    2, 4, RB, hi - lo
                ).astype(BF)
            return carry

        lax.fori_loop(0, 4, step, 0)

    def ring(o):
        return cx if o == 0 else cy

    def on_first(o, i):
        return place(i, cy, cz) if o == 0 else place(cx, i, cz)

    def on_second(o, i):
        return place(cx, i, cz) if o == 0 else place(i, cy, cz)

    def remote(src, dst, ssem, rsem, to):
        return pltpu.make_async_remote_copy(
            src_ref=src, dst_ref=dst, send_sem=ssem, recv_sem=rsem, device_id=to, device_id_type=MESH
        )

    def first_copies(sec, o):
        i = ring(o)
        up, dn, opp = lax.rem(i + 1, 4), lax.rem(i + 3, 4), lax.rem(i + 2, 4)
        g = m.grad
        one = [
            remote(g.at[sec, o * 4 + opp, 0:2], m.r1.at[sec, o, 0],
                   m.r1_s_sem.at[sec, o, 0], m.r1_r_sem.at[sec, o, 0], on_first(o, up)),
            remote(g.at[sec, o * 4 + opp, 2:4], m.r1.at[sec, o, 1],
                   m.r1_s_sem.at[sec, o, 1], m.r1_r_sem.at[sec, o, 1], on_first(o, dn)),
        ]
        two = [
            [
                remote(g.at[sec, o * 4 + up, 2 * b: 2 * b + 2], m.r2.at[sec, o, 0, 2 * b: 2 * b + 2],
                       m.r2_s_sem.at[sec, o, 0, b], m.r2_r_sem.at[sec, o, 0, b], on_first(o, up))
                for b in range(2)
            ],
            [
                remote(g.at[sec, o * 4 + dn, 2 * b: 2 * b + 2], m.r2.at[sec, o, 1, 2 * b: 2 * b + 2],
                       m.r2_s_sem.at[sec, o, 1, b], m.r2_r_sem.at[sec, o, 1, b], on_first(o, dn))
                for b in range(2)
            ],
        ]
        return one, two, up, dn, i

    def reduce_start(sec):
        for o in range(2):
            one, two, up, dn, i = first_copies(sec, o)
            one[0].start()
            one[1].start()
            two[0][1].start()
            two[1][0].start()

    def reduce_relay(sec):
        for o in range(2):
            one, two, up, dn, i = first_copies(sec, o)
            for side, chunk, b in ((0, up, 0), (1, dn, 1)):
                one[side].wait_recv()
                for e in range(2 * b, 2 * b + 2):
                    acc = m.grad[sec, o * 4 + chunk, e].astype(F32)
                    acc = acc + m.r1[sec, o, side, e - 2 * b].astype(F32)
                    m.grad[sec, o * 4 + chunk, e] = acc.astype(BF)
                two[side][b].start()

    def second_copies(sec, o):
        j = ring(1 - o)
        return [
            remote(m.hsum.at[sec, o, lax.rem(j + d, 4)], m.r3.at[sec, o, d - 1],
                   m.r3_s_sem.at[sec, o, d - 1], m.r3_r_sem.at[sec, o, d - 1],
                   on_second(o, lax.rem(j + d, 4)))
            for d in (1, 2, 3)
        ]

    def reduce_second(sec):
        for o in range(2):
            one, two, up, dn, i = first_copies(sec, o)
            for side in two:
                for c in side:
                    c.wait_recv()
            for e in range(4):
                acc = m.grad[sec, o * 4 + i, e].astype(F32)
                acc = acc + m.r2[sec, o, 0, e].astype(F32)
                acc = acc + m.r2[sec, o, 1, e].astype(F32)
                m.hsum[sec, o, e] = acc.astype(BF)
            for c in second_copies(sec, o):
                c.start()

    def z_copies(sec):
        copies = []
        for d in (1, 2, 3):
            z = lax.rem(cz + d, 4)
            copies.append(
                remote(m.zsum.at[sec, lax.rem(z, 2), z // 2], m.r4.at[sec, d - 1],
                       m.r4_s_sem.at[sec, d - 1], m.r4_r_sem.at[sec, d - 1], place(cx, cy, z))
            )
        return copies

    def reduce_z(sec):
        for o in range(2):
            for c in second_copies(sec, o):
                c.wait_recv()
            acc = m.hsum[sec, o, ring(1 - o)].astype(F32)
            for d in range(3):
                acc = acc + m.r3[sec, o, d].astype(F32)
            for z in range(2):
                m.zsum[sec, o, z] = jnp.concatenate(
                    [acc[:, 432 * z: 432 * (z + 1)], acc[:, 864 + 144 * z: 864 + 144 * (z + 1)]],
                    axis=1,
                ).astype(BF)
        for c in z_copies(sec):
            c.start()

    def reduce_end(sec, gq, gout):
        for c in z_copies(sec):
            c.wait_recv()
        acc = m.zsum[sec, zl, zh].astype(F32)
        for d in range(3):
            acc = acc + m.r4[sec, d].astype(F32)
        gq[...] = acc[0:36, 0:432]
        gout[...] = acc[0:36, 432:576]

    def reduce_drain(sec):
        for c in core_copies(sec)[2:]:
            c.wait_send()
        for o in range(2):
            one, two, up, dn, i = first_copies(sec, o)
            for c in one + two[0] + two[1]:
                c.wait_send()
            for c in second_copies(sec, o):
                c.wait_send()
        for c in z_copies(sec):
            c.wait_send()

    loads[0].wait()
    normalize(m.x, m.normed_s)
    pl.semaphore_wait(barrier, NS + 2)
    a2a_start(0, ins[1], m.go)
    own = pltpu.make_async_copy(ins[1].at[me], m.go.at[me], m.load_sem.at[1])
    own.start()
    loads[4].wait()
    qkv_heads(m.normed_s, m.wqs, m.hs_s)

    def spatial_head(h, carry):
        p = softmax(m.hs_s[h], m.hs_s[h + 8], None)
        m.probs[h] = p
        m.mh_s[h] = nn(p.astype(BF), m.hs_s[h + 16]).astype(BF)
        return carry

    lax.fori_loop(0, H, spatial_head, 0)
    for h in range(H):
        m.mixed[:, HD * h: HD * (h + 1)] = m.mh_s[h][:, :HD]
    loads[2].wait()
    loads[5].wait()
    for n in range(3):
        c = slice(384 * n, 384 * (n + 1))
        proj = nt(m.mixed[...], m.wos[c, :]).reshape(32, 8, 384)
        keep = m.ks[:, :, c].astype(F32) * KEEP
        m.y_out[:, :, c] = (m.x[:, :, c].astype(F32) + proj * keep).astype(BF)
    a2a_start(1, m.y_out, m.y_in)
    m.y_in[me] = m.y_out[me]

    def perm_step(n, carry):
        blocks = []
        for k in (2 * n, 2 * n + 1):
            o, a, b = k // 16, lax.rem(k // 4, 4), lax.rem(k, 4)
            x = a * (1 - o) + b * o
            y = b * (1 - o) + a * o
            s = x * 8 + o * 4 + y
            row = lax.broadcasted_iota(jnp.int32, (RB, D), 0)
            col = lax.broadcasted_iota(jnp.int32, (RB, D), 1)
            hit = (col == row + 36 * s) & (row < 36)
            blocks.append(jnp.where(hit, 1.0, 0.0))
        both = jnp.concatenate(blocks, axis=0).astype(BF)
        m.perm[pl.ds(pl.multiple_of(n * 80, 80), 80), :] = both
        return carry

    lax.fori_loop(0, NS // 2, perm_step, 0)

    own.wait()
    a2a_wait(0, m.go, m.go)
    loads[3].wait()
    loads[7].wait()
    d_proj_mix(m.go, m.kt, m.wot)
    transpose_rows(1, m.dproj)
    core_copies(0)[1].start()
    a2a_wait(1, m.y_out, m.y_in)
    normalize(m.y_in, m.normed_t)
    loads[6].wait()
    qkv_heads(m.normed_t, m.wqt, m.hs_t)

    def temporal_head(h, carry):
        i = lax.broadcasted_iota(jnp.int32, (T, T), 0)
        j = lax.broadcasted_iota(jnp.int32, (T, T), 1)
        mask = ((i - j) & 7) == 0
        q, k, v = m.hs_t[h], m.hs_t[h + 8], m.hs_t[h + 16]
        p = softmax(q, k, mask)
        p_low = p.astype(BF)
        m.mh_t[h] = nn(p_low, v).astype(BF)
        attention_backward(h, p, p_low, q, k, v)
        return carry

    lax.fori_loop(0, H, temporal_head, 0)
    gather_columns(0, m.mh_t)
    core_copies(0)[2].start()
    input_backward(m.y_in, m.go, m.d_out, m.wqt)
    a2a_start(2, m.d_out, m.d_in)
    m.d_in[me] = m.d_out[me]
    transpose_rows(0, m.normed_t)
    core_copies(0)[0].start()
    for c in core_copies(0):
        c.wait_recv()
    weight_grads(0)
    for c in core_copies(0)[:2]:
        c.wait_send()

    transpose_rows(0, m.normed_s)
    core_copies(1)[0].start()
    a2a_wait(2, m.d_out, m.d_in)
    reduce_start(0)
    d_proj_mix(m.d_in, m.ks, m.wos)
    transpose_rows(1, m.dproj)
    core_copies(1)[1].start()
    reduce_relay(0)

    def spatial_back(h, carry):
        p = m.probs[h]
        attention_backward(h, p, p.astype(BF), m.hs_s[h], m.hs_s[h + 8], m.hs_s[h + 16])
        return carry

    lax.fori_loop(0, H, spatial_back, 0)
    gather_columns(1, m.mh_s)
    core_copies(1)[2].start()
    reduce_second(0)
    for c in core_copies(1):
        c.wait_recv()
    weight_grads(1)
    reduce_start(1)
    reduce_z(0)
    input_backward(m.x, m.d_in, m.dx, m.wqs)
    store = pltpu.make_async_copy(m.dx, dx_hbm, m.store_sem.at[0])
    store.start()
    reduce_end(0, gqt, got)
    reduce_relay(1)
    reduce_second(1)
    reduce_z(1)
    reduce_end(1, gqs, gos)

    a2a_drain(0, ins[1], m.go)
    a2a_drain(1, m.y_out, m.y_in)
    a2a_drain(2, m.d_out, m.d_in)
    for c in core_copies(1)[:2]:
        c.wait_send()
    reduce_drain(0)
    reduce_drain(1)
    store.wait()


def shards(
    block_input,
    out_grad,
    spatial_keep,
    temporal_keep,
    spatial_qkv,
    spatial_out,
    temporal_qkv,
    temporal_out,
):
    hbm = pl.BlockSpec(memory_space=pl.ANY)
    vmem = pl.BlockSpec(memory_space=pltpu.VMEM)
    outs = pl.pallas_call(
        body,
        out_shape=(
            jax.ShapeDtypeStruct((32, 8, D), BF),
            jax.ShapeDtypeStruct((36, 432), F32),
            jax.ShapeDtypeStruct((36, 144), F32),
            jax.ShapeDtypeStruct((36, 432), F32),
            jax.ShapeDtypeStruct((36, 144), F32),
        ),
        in_specs=[hbm] * 8,
        out_specs=(hbm, vmem, vmem, vmem, vmem),
        scratch_shapes=[pltpu.VMEM(s, d) for s, d in SCRATCH.values()]
        + [pltpu.SemaphoreType.DMA(s) for s in SEMS.values()],
        compiler_params=pltpu.CompilerParams(
            collective_id=0, has_side_effects=True, vmem_limit_bytes=63 * 2**20
        ),
    )(
        block_input.reshape(32, 8, D),
        out_grad.reshape(32, 8, D),
        spatial_keep.reshape(32, 8, D),
        temporal_keep.reshape(32, 8, D),
        spatial_qkv,
        spatial_out,
        temporal_qkv,
        temporal_out,
    )
    return (outs[0].reshape(1, 1, T, D),) + tuple(outs[1:])


def solution(mesh):
    return jax.shard_map(
        shards,
        mesh=mesh,
        in_specs=(
            P("dp", "seq", None, None),
            P("dp", "seq", None, None),
            P("dp", "seq", None, None),
            P("dp", None, "seq", None),
            P(),
            P(),
            P(),
            P(),
        ),
        out_specs=(
            P("dp", "seq", None, None),
            P("seq", "dp"),
            P("seq", "dp"),
            P("seq", "dp"),
            P("seq", "dp"),
        ),
        check_vma=False,
    )
```

```python
import jax
import jax.numpy as jnp
from jax import lax
from jax.experimental import pallas as pl
from jax.experimental.pallas import tpu as pltpu
from jax.sharding import PartitionSpec as P

D = 1152
H = 8
HD = 72
INNER = 576
T = 256
NS = 32
RB = 40
MESH = pl.DeviceIdType.MESH
BF = jnp.bfloat16
F32 = jnp.float32
SCALE = HD ** (-0.5)
KEEP = 1.0 / 0.9


def nt(a, b):
    return lax.dot_general(a, b, (((1,), (1,)), ((), ())), preferred_element_type=F32)


def tn(a, b):
    return lax.dot_general(a, b, (((0,), (0,)), ((), ())), preferred_element_type=F32)


def nn(a, b):
    return jnp.dot(a, b, preferred_element_type=F32)


SCRATCH = dict(
    x=((32, 8, D), BF),
    ks=((32, 8, D), jnp.int32),
    kt=((32, 8, D), jnp.int32),
    wqs=((3 * INNER, D), BF),
    wos=((INNER, D), BF),
    wqt=((3 * INNER, D), BF),
    wot=((INNER, D), BF),
    go=((NS, 8, D), BF),
    y_out=((NS, 8, D), BF),
    y_in=((NS, 8, D), BF),
    d_out=((NS, 8, D), BF),
    d_in=((NS, 8, D), BF),
    normed_s=((T, D), BF),
    normed_t=((T, D), BF),
    hs_s=((24, HD, T), BF),
    hs_t=((24, HD, T), BF),
    probs=((H, T, T), F32),
    mh_s=((H, HD, T), BF),
    mh_t=((H, HD, T), BF),
    mixed=((T, INNER), BF),
    dproj=((T, D), BF),
    dmh=((H, HD, T), BF),
    dh=((24, HD, T), BF),
    dqkv=((T, 3 * INNER), BF),
    dn=((T, D), F32),
    dsel=((2, 2, D, T), BF),
    dsel_in=((2, D, T), BF),
    perm=((32 * RB, D), BF),
    lt=((2, 32 * RB, T), BF),
    lt_in=((2, 2, 32 * RB, T), BF),
    grad=((2, 8, 4, RB, D), BF),
    r1=((2, 2, 2, 2, RB, D), BF),
    r2=((2, 2, 2, 4, RB, D), BF),
    hsum=((2, 2, 4, RB, D), BF),
    r3=((2, 2, 3, RB, D), BF),
    zsum=((2, 2, 2, RB, INNER), BF),
    r4=((2, 3, RB, INNER), BF),
    dx=((32, 8, D), BF),
)
SEMS = dict(
    load=(8,),
    store=(1,),
    a2a_s=(3, 31),
    a2a_r=(3, 31),
    core_s=(2, 3),
    core_r=(2, 3),
    r1_s=(2, 2, 2),
    r1_r=(2, 2, 2),
    r2_s=(2, 2, 2, 2),
    r2_r=(2, 2, 2, 2),
    r3_s=(2, 2, 3),
    r3_r=(2, 2, 3),
    r4_s=(2, 3),
    r4_r=(2, 3),
)


class Refs:
    pass


def body(*refs):
    ins, outs, rest = refs[:8], refs[8:13], refs[13:]
    m = Refs()
    for name, ref in zip(SCRATCH, rest[: len(SCRATCH)]):
        setattr(m, name, ref)
    for name, ref in zip(SEMS, rest[len(SCRATCH):]):
        setattr(m, name + "_sem", ref)
    dx_hbm, gqs, gos, gqt, got = outs

    dp = lax.axis_index("dp")
    me = lax.axis_index("seq")
    zh, core = dp // 2, lax.rem(dp, 2)
    cx, zl, cy = me // 8, lax.rem(me // 4, 2), lax.rem(me, 4)
    cz = zh * 2 + zl

    def place(x, y, z):
        return ((z // 2) * 2 + core, x * 8 + lax.rem(z, 2) * 4 + y)

    dests = (m.x, None, m.ks, m.kt, m.wqs, m.wos, m.wqt, m.wot)
    loads = [
        None if dst is None else pltpu.make_async_copy(src, dst, m.load_sem.at[i])
        for i, (src, dst) in enumerate(zip(ins, dests))
    ]
    for i in (0, 4, 2, 5, 7, 3, 6):
        loads[i].start()

    barrier = pltpu.get_barrier_semaphore()

    def greet(d, carry):
        pl.semaphore_signal(
            barrier, inc=1, device_id=(dp, lax.rem(me + d, NS)), device_id_type=MESH
        )
        return carry

    lax.fori_loop(1, NS, greet, 0)
    other_core = (zh * 2 + 1 - core, me)
    pl.semaphore_signal(barrier, inc=1, device_id=other_core, device_id_type=MESH)
    far = (1 - zh) * 2 + core
    pl.semaphore_signal(barrier, inc=1, device_id=(far, me), device_id_type=MESH)
    pl.semaphore_signal(
        barrier, inc=1, device_id=(far, cx * 8 + (1 - zl) * 4 + cy), device_id_type=MESH
    )

    def a2a_copy(k, src, dst, d):
        to = lax.rem(me + d, NS)
        return pltpu.make_async_remote_copy(
            src_ref=src.at[to],
            dst_ref=dst.at[me],
            send_sem=m.a2a_s_sem.at[k, d - 1],
            recv_sem=m.a2a_r_sem.at[k, d - 1],
            device_id=(dp, to),
            device_id_type=MESH,
        )

    def a2a_start(k, src, dst):
        def step(d, carry):
            a2a_copy(k, src, dst, d).start()
            return carry

        lax.fori_loop(1, NS, step, 0)

    def a2a_wait(k, src, dst):
        def step(d, carry):
            frm = lax.rem(me + NS - d, NS)
            pltpu.make_async_remote_copy(
                src_ref=src.at[frm],
                dst_ref=dst.at[frm],
                send_sem=m.a2a_s_sem.at[k, d - 1],
                recv_sem=m.a2a_r_sem.at[k, d - 1],
                device_id=(dp, frm),
                device_id_type=MESH,
            ).wait_recv()
            return carry

        lax.fori_loop(1, NS, step, 0)

    def a2a_drain(k, src, dst):
        def step(d, carry):
            a2a_copy(k, src, dst, d).wait_send()
            return carry

        lax.fori_loop(1, NS, step, 0)

    def rows(fn):
        def step(r, carry):
            fn(pl.ds(pl.multiple_of(r * 32, 32), 32), pl.ds(r * 4, 4))
            return carry

        lax.fori_loop(0, 8, step, 0)

    def flat(ref, blk):
        return ref[blk].astype(F32).reshape(32, D)

    def inv_of(zf):
        return lax.rsqrt(jnp.mean(zf * zf, axis=-1, keepdims=True) + 1e-06)

    def normalize(src, dst):
        def fn(r, blk):
            zf = flat(src, blk)
            dst[r, :] = (zf * inv_of(zf)).astype(BF)

        rows(fn)

    def heads(ref, js):
        return jnp.concatenate([ref[j].astype(F32) for j in js], axis=0)

    def qkv_heads(normed, w, hs):
        for n in range(3):
            part = nt(w[INNER * n: INNER * (n + 1), :], normed[...])
            hs[H * n: H * (n + 1)] = part.reshape(H, HD, T).astype(BF)

    def d_proj_mix(dy, keep, wo):
        def fn(r, blk):
            m.dproj[r, :] = (flat(dy, blk) * (flat(keep, blk) * KEEP)).astype(BF)

        rows(fn)
        m.dmh[...] = nt(wo[...], m.dproj[...]).reshape(H, HD, T).astype(BF)

    def softmax(q, k, mask):
        e = jnp.exp(tn(q, k) * SCALE)
        if mask is not None:
            e = jnp.where(mask, e, 0.0)
        return e * (1.0 / jnp.sum(e, axis=-1, keepdims=True))

    def attention_backward(h, p, p_low, q, k, v):
        dm = m.dmh[h]
        dp_ = tn(dm, v)
        ds = (p * (dp_ - jnp.sum(p * dp_, axis=-1, keepdims=True)) * SCALE).astype(BF)
        m.dh[h] = nt(k, ds).astype(BF)
        m.dh[h + 8] = nn(q, ds).astype(BF)
        m.dh[h + 16] = nn(dm, p_low).astype(BF)

    def gather_columns(sec, mh):
        for c in range(2):
            js = [6 * c + i for i in range(6)] + [12 + 6 * c + i for i in range(6)]
            hs = (2 * c, 2 * c + 1, 4 + 2 * c, 5 + 2 * c)
            both = jnp.concatenate([heads(m.dh, js), heads(mh, hs)], axis=0)
            m.dsel[sec, c] = both.astype(BF)

    def input_backward(src, dy, dst, wq):
        m.dqkv[:, 0:1152] = heads(m.dh, range(16)).T.astype(BF)
        m.dqkv[:, 1152:1728] = heads(m.dh, range(16, 24)).T.astype(BF)
        for n in range(3):
            m.dn[:, 384 * n: 384 * (n + 1)] = nn(m.dqkv[...], wq[:, 384 * n: 384 * (n + 1)])

        def fn(r, blk):
            zf = flat(src, blk)
            inv = inv_of(zf)
            c = zf * inv
            dn = m.dn[r, :]
            dz = flat(dy, blk) + inv * (dn - c * jnp.mean(dn * c, axis=-1, keepdims=True))
            dst[blk] = dz.reshape(4, 8, D).astype(BF)

        rows(fn)

    def core_copies(sec):
        pairs = (
            (m.lt.at[0], m.lt_in.at[sec, 0]),
            (m.lt.at[1], m.lt_in.at[sec, 1]),
            (m.dsel.at[sec, 1 - core], m.dsel_in.at[sec]),
        )
        return [
            pltpu.make_async_remote_copy(
                src_ref=src,
                dst_ref=dst,
                send_sem=m.core_s_sem.at[sec, i],
                recv_sem=m.core_r_sem.at[sec, i],
                device_id=other_core,
                device_id_type=MESH,
            )
            for i, (src, dst) in enumerate(pairs)
        ]

    def transpose_rows(i, src):
        def step(n, carry):
            r = pl.ds(pl.multiple_of(n * 320, 320), 320)
            m.lt[i, r, :] = nt(m.perm[r, :], src[...]).astype(BF)
            return carry

        lax.fori_loop(0, 4, step, 0)

    def weight_grads(sec):
        def step(n, carry):
            r = pl.ds(pl.multiple_of(n * 320, 320), 320)
            for i, lo, hi in ((0, 0, 384), (0, 384, 864), (1, 864, 1152)):
                acc = nt(m.lt[i, r, :], m.dsel[sec, core, lo:hi, :])
                acc = acc + nt(m.lt_in[sec, i, r, :], m.dsel_in[sec, lo:hi, :])
                m.grad[sec, pl.ds(n * 2, 2), :, :, lo:hi] = acc.reshape(
                    2, 4, RB, hi - lo
                ).astype(BF)
            return carry

        lax.fori_loop(0, 4, step, 0)

    def ring(o):
        return cx if o == 0 else cy

    def on_first(o, i):
        return place(i, cy, cz) if o == 0 else place(cx, i, cz)

    def on_second(o, i):
        return place(cx, i, cz) if o == 0 else place(i, cy, cz)

    def remote(src, dst, ssem, rsem, to):
        return pltpu.make_async_remote_copy(
            src_ref=src, dst_ref=dst, send_sem=ssem, recv_sem=rsem, device_id=to, device_id_type=MESH
        )

    def first_copies(sec, o):
        i = ring(o)
        up, dn, opp = lax.rem(i + 1, 4), lax.rem(i + 3, 4), lax.rem(i + 2, 4)
        g = m.grad
        one = [
            remote(g.at[sec, o * 4 + opp, 0:2], m.r1.at[sec, o, 0],
                   m.r1_s_sem.at[sec, o, 0], m.r1_r_sem.at[sec, o, 0], on_first(o, up)),
            remote(g.at[sec, o * 4 + opp, 2:4], m.r1.at[sec, o, 1],
                   m.r1_s_sem.at[sec, o, 1], m.r1_r_sem.at[sec, o, 1], on_first(o, dn)),
        ]
        two = [
            [
                remote(g.at[sec, o * 4 + up, 2 * b: 2 * b + 2], m.r2.at[sec, o, 0, 2 * b: 2 * b + 2],
                       m.r2_s_sem.at[sec, o, 0, b], m.r2_r_sem.at[sec, o, 0, b], on_first(o, up))
                for b in range(2)
            ],
            [
                remote(g.at[sec, o * 4 + dn, 2 * b: 2 * b + 2], m.r2.at[sec, o, 1, 2 * b: 2 * b + 2],
                       m.r2_s_sem.at[sec, o, 1, b], m.r2_r_sem.at[sec, o, 1, b], on_first(o, dn))
                for b in range(2)
            ],
        ]
        return one, two, up, dn, i

    def reduce_start(sec):
        for o in range(2):
            one, two, up, dn, i = first_copies(sec, o)
            one[0].start()
            one[1].start()
            two[0][1].start()
            two[1][0].start()

    def reduce_relay(sec):
        for o in range(2):
            one, two, up, dn, i = first_copies(sec, o)
            for side, chunk, b in ((0, up, 0), (1, dn, 1)):
                one[side].wait_recv()
                for e in range(2 * b, 2 * b + 2):
                    acc = m.grad[sec, o * 4 + chunk, e].astype(F32)
                    acc = acc + m.r1[sec, o, side, e - 2 * b].astype(F32)
                    m.grad[sec, o * 4 + chunk, e] = acc.astype(BF)
                two[side][b].start()

    def second_copies(sec, o):
        j = ring(1 - o)
        return [
            remote(m.hsum.at[sec, o, lax.rem(j + d, 4)], m.r3.at[sec, o, d - 1],
                   m.r3_s_sem.at[sec, o, d - 1], m.r3_r_sem.at[sec, o, d - 1],
                   on_second(o, lax.rem(j + d, 4)))
            for d in (1, 2, 3)
        ]

    def reduce_second(sec):
        for o in range(2):
            one, two, up, dn, i = first_copies(sec, o)
            for side in two:
                for c in side:
                    c.wait_recv()
            for e in range(4):
                acc = m.grad[sec, o * 4 + i, e].astype(F32)
                acc = acc + m.r2[sec, o, 0, e].astype(F32)
                acc = acc + m.r2[sec, o, 1, e].astype(F32)
                m.hsum[sec, o, e] = acc.astype(BF)
            for c in second_copies(sec, o):
                c.start()

    def z_copies(sec):
        copies = []
        for d in (1, 2, 3):
            z = lax.rem(cz + d, 4)
            copies.append(
                remote(m.zsum.at[sec, lax.rem(z, 2), z // 2], m.r4.at[sec, d - 1],
                       m.r4_s_sem.at[sec, d - 1], m.r4_r_sem.at[sec, d - 1], place(cx, cy, z))
            )
        return copies

    def reduce_z(sec):
        for o in range(2):
            for c in second_copies(sec, o):
                c.wait_recv()
            acc = m.hsum[sec, o, ring(1 - o)].astype(F32)
            for d in range(3):
                acc = acc + m.r3[sec, o, d].astype(F32)
            for z in range(2):
                m.zsum[sec, o, z] = jnp.concatenate(
                    [acc[:, 432 * z: 432 * (z + 1)], acc[:, 864 + 144 * z: 864 + 144 * (z + 1)]],
                    axis=1,
                ).astype(BF)
        for c in z_copies(sec):
            c.start()

    def reduce_end(sec, gq, gout):
        for c in z_copies(sec):
            c.wait_recv()
        acc = m.zsum[sec, zl, zh].astype(F32)
        for d in range(3):
            acc = acc + m.r4[sec, d].astype(F32)
        gq[...] = acc[0:36, 0:432]
        gout[...] = acc[0:36, 432:576]

    def reduce_drain(sec):
        for c in core_copies(sec)[2:]:
            c.wait_send()
        for o in range(2):
            one, two, up, dn, i = first_copies(sec, o)
            for c in one + two[0] + two[1]:
                c.wait_send()
            for c in second_copies(sec, o):
                c.wait_send()
        for c in z_copies(sec):
            c.wait_send()

    loads[0].wait()
    normalize(m.x, m.normed_s)
    pl.semaphore_wait(barrier, NS + 2)
    a2a_start(0, ins[1], m.go)
    own = pltpu.make_async_copy(ins[1].at[me], m.go.at[me], m.load_sem.at[1])
    own.start()
    loads[4].wait()
    qkv_heads(m.normed_s, m.wqs, m.hs_s)

    def spatial_head(h, carry):
        p = softmax(m.hs_s[h], m.hs_s[h + 8], None)
        m.probs[h] = p
        m.mh_s[h] = nt(m.hs_s[h + 16], p.astype(BF)).astype(BF)
        return carry

    lax.fori_loop(0, H, spatial_head, 0)
    m.mixed[...] = heads(m.mh_s, range(H)).T.astype(BF)
    loads[2].wait()
    loads[5].wait()
    for n in range(3):
        c = slice(384 * n, 384 * (n + 1))
        proj = nn(m.mixed[...], m.wos[:, c]).reshape(32, 8, 384)
        keep = m.ks[:, :, c].astype(F32) * KEEP
        m.y_out[:, :, c] = (m.x[:, :, c].astype(F32) + proj * keep).astype(BF)
    a2a_start(1, m.y_out, m.y_in)
    m.y_in[me] = m.y_out[me]

    def perm_step(n, carry):
        blocks = []
        for k in (2 * n, 2 * n + 1):
            o, a, b = k // 16, lax.rem(k // 4, 4), lax.rem(k, 4)
            x = a * (1 - o) + b * o
            y = b * (1 - o) + a * o
            s = x * 8 + o * 4 + y
            row = lax.broadcasted_iota(jnp.int32, (RB, D), 0)
            col = lax.broadcasted_iota(jnp.int32, (RB, D), 1)
            hit = (col == row + 36 * s) & (row < 36)
            blocks.append(jnp.where(hit, 1.0, 0.0))
        both = jnp.concatenate(blocks, axis=0).astype(BF)
        m.perm[pl.ds(pl.multiple_of(n * 80, 80), 80), :] = both
        return carry

    lax.fori_loop(0, NS // 2, perm_step, 0)

    own.wait()
    a2a_wait(0, m.go, m.go)
    loads[3].wait()
    loads[7].wait()
    d_proj_mix(m.go, m.kt, m.wot)
    transpose_rows(1, m.dproj)
    core_copies(0)[1].start()
    a2a_wait(1, m.y_out, m.y_in)
    normalize(m.y_in, m.normed_t)
    loads[6].wait()
    qkv_heads(m.normed_t, m.wqt, m.hs_t)

    def temporal_head(h, carry):
        i = lax.broadcasted_iota(jnp.int32, (T, T), 0)
        j = lax.broadcasted_iota(jnp.int32, (T, T), 1)
        mask = ((i - j) & 7) == 0
        q, k, v = m.hs_t[h], m.hs_t[h + 8], m.hs_t[h + 16]
        p = softmax(q, k, mask)
        p_low = p.astype(BF)
        m.mh_t[h] = nt(v, p_low).astype(BF)
        attention_backward(h, p, p_low, q, k, v)
        return carry

    lax.fori_loop(0, H, temporal_head, 0)
    gather_columns(0, m.mh_t)
    core_copies(0)[2].start()
    input_backward(m.y_in, m.go, m.d_out, m.wqt)
    a2a_start(2, m.d_out, m.d_in)
    m.d_in[me] = m.d_out[me]
    transpose_rows(0, m.normed_t)
    core_copies(0)[0].start()
    for c in core_copies(0):
        c.wait_recv()
    weight_grads(0)
    for c in core_copies(0)[:2]:
        c.wait_send()

    transpose_rows(0, m.normed_s)
    core_copies(1)[0].start()
    a2a_wait(2, m.d_out, m.d_in)
    reduce_start(0)
    d_proj_mix(m.d_in, m.ks, m.wos)
    transpose_rows(1, m.dproj)
    core_copies(1)[1].start()
    reduce_relay(0)

    def spatial_back(h, carry):
        p = m.probs[h]
        attention_backward(h, p, p.astype(BF), m.hs_s[h], m.hs_s[h + 8], m.hs_s[h + 16])
        return carry

    lax.fori_loop(0, H, spatial_back, 0)
    gather_columns(1, m.mh_s)
    core_copies(1)[2].start()
    reduce_second(0)
    for c in core_copies(1):
        c.wait_recv()
    weight_grads(1)
    reduce_start(1)
    reduce_z(0)
    input_backward(m.x, m.d_in, m.dx, m.wqs)
    store = pltpu.make_async_copy(m.dx, dx_hbm, m.store_sem.at[0])
    store.start()
    reduce_end(0, gqt, got)
    reduce_relay(1)
    reduce_second(1)
    reduce_z(1)
    reduce_end(1, gqs, gos)

    a2a_drain(0, ins[1], m.go)
    a2a_drain(1, m.y_out, m.y_in)
    a2a_drain(2, m.d_out, m.d_in)
    for c in core_copies(1)[:2]:
        c.wait_send()
    reduce_drain(0)
    reduce_drain(1)
    store.wait()


def hand_over(*refs):
    sem = refs[10]
    copies = [pltpu.make_async_copy(refs[i], refs[5 + i], sem.at[i]) for i in range(5)]
    for c in copies:
        c.start()
    for c in copies:
        c.wait()


def shards(
    block_input,
    out_grad,
    spatial_keep,
    temporal_keep,
    spatial_qkv,
    spatial_out,
    temporal_qkv,
    temporal_out,
):
    hbm = pl.BlockSpec(memory_space=pl.ANY)
    vmem = pl.BlockSpec(memory_space=pltpu.VMEM)
    outs = pl.pallas_call(
        body,
        out_shape=(
            jax.ShapeDtypeStruct((32, 8, D), BF),
            jax.ShapeDtypeStruct((36, 432), F32),
            jax.ShapeDtypeStruct((36, 144), F32),
            jax.ShapeDtypeStruct((36, 432), F32),
            jax.ShapeDtypeStruct((36, 144), F32),
        ),
        in_specs=[hbm] * 8,
        out_specs=(hbm, vmem, vmem, vmem, vmem),
        scratch_shapes=[pltpu.VMEM(s, d) for s, d in SCRATCH.values()]
        + [pltpu.SemaphoreType.DMA(s) for s in SEMS.values()],
        compiler_params=pltpu.CompilerParams(
            collective_id=0, has_side_effects=True, vmem_limit_bytes=63 * 2**20
        ),
    )(
        block_input.reshape(32, 8, D),
        out_grad.reshape(32, 8, D),
        spatial_keep.reshape(32, 8, D),
        temporal_keep.reshape(32, 8, D),
        spatial_qkv.T,
        spatial_out.T,
        temporal_qkv.T,
        temporal_out.T,
    )
    outs = pl.pallas_call(
        hand_over,
        out_shape=tuple(jax.ShapeDtypeStruct(o.shape, o.dtype) for o in outs),
        in_specs=[vmem] * 5,
        out_specs=(hbm,) * 5,
        scratch_shapes=[pltpu.SemaphoreType.DMA((5,))],
    )(*outs)
    return (outs[0].reshape(1, 1, T, D),) + tuple(outs[1:])


def solution(mesh):
    return jax.shard_map(
        shards,
        mesh=mesh,
        in_specs=(
            P("dp", "seq", None, None),
            P("dp", "seq", None, None),
            P("dp", "seq", None, None),
            P("dp", None, "seq", None),
            P(),
            P(),
            P(),
            P(),
        ),
        out_specs=(
            P("dp", "seq", None, None),
            P("seq", "dp"),
            P("seq", "dp"),
            P("seq", "dp"),
            P("seq", "dp"),
        ),
        check_vma=False,
    )
```

```python
import jax
import jax.numpy as jnp
from jax import lax
from jax.experimental import pallas as pl
from jax.experimental.pallas import tpu as pltpu
from jax.sharding import PartitionSpec as P

D = 1152
H = 8
HD = 72
INNER = 576
T = 256
NS = 32
RB = 40
MESH = pl.DeviceIdType.MESH
BF = jnp.bfloat16
F32 = jnp.float32
SCALE = HD ** (-0.5)
KEEP = 1.0 / 0.9


def nt(a, b):
    return lax.dot_general(a, b, (((1,), (1,)), ((), ())), preferred_element_type=F32)


def tn(a, b):
    return lax.dot_general(a, b, (((0,), (0,)), ((), ())), preferred_element_type=F32)


def nn(a, b):
    return jnp.dot(a, b, preferred_element_type=F32)


SCRATCH = dict(
    x=((32, 8, D), BF),
    ks=((32, 8, D), jnp.int32),
    kt=((32, 8, D), jnp.int32),
    wqs=((3 * INNER, D), BF),
    wos=((INNER, D), BF),
    wqt=((3 * INNER, D), BF),
    wot=((INNER, D), BF),
    go=((NS, 8, D), BF),
    y_out=((NS, 8, D), BF),
    y_in=((NS, 8, D), BF),
    d_out=((NS, 8, D), BF),
    d_in=((NS, 8, D), BF),
    normed_s=((T, D), BF),
    normed_t=((T, D), BF),
    hs_s=((24, HD, T), BF),
    hs_t=((24, HD, T), BF),
    probs=((H, T, T), F32),
    mh_s=((H, HD, T), BF),
    mh_t=((H, HD, T), BF),
    mixed=((T, INNER), BF),
    dproj=((T, D), BF),
    dmh=((H, HD, T), BF),
    dh=((24, HD, T), BF),
    dqkv=((T, 3 * INNER), BF),
    dn=((T, D), F32),
    dsel=((2, 2, D, T), BF),
    dsel_in=((2, D, T), BF),
    perm=((32 * RB, D), BF),
    lt=((2, 2, 32 * RB, T), BF),
    lt_in=((2, 2, 32 * RB, T), BF),
    dx=((32, 8, D), BF),
)
SEMS = dict(
    load=(8,),
    store=(1,),
    a2a_s=(3, 31),
    a2a_r=(3, 31),
    core_s=(2, 4),
    core_r=(2, 4),
)
BATCHES = dict(time=(896, 512, True), out=(384, 256, False), space=(640, 384, True))
for _n, (_w, _z, _c) in BATCHES.items():
    SCRATCH.update({
        _n + "_g": ((8, 4, RB, _w), BF),
        _n + "_r1": ((2, 2, 2, RB, _w), BF),
        _n + "_r2": ((2, 2, 4, RB, _w), BF),
        _n + "_h": ((2, 4, RB, _w), BF),
        _n + "_r3": ((2, 3, RB, _w), BF),
        _n + "_z": ((2, 2, RB, _z), BF),
        _n + "_r4": ((3, RB, _z), BF),
    })
    SEMS.update({
        _n + "_r1_s": (2, 2), _n + "_r1_r": (2, 2), _n + "_r2_s": (2, 2, 2), _n + "_r2_r": (2, 2, 2),
        _n + "_r3_s": (2, 3), _n + "_r3_r": (2, 3), _n + "_r4_s": (3,), _n + "_r4_r": (3,),
    })
    if _c:
        SCRATCH.update({
            _n + "_c": ((2, 2, 4, 4, RB, 128), BF),
            _n + "_ci": ((3, 4, 4, RB, 128), BF),
            _n + "_cs": ((4, 4, RB, 128), BF),
            _n + "_cj": ((15, RB, 128), BF),
        })
        SEMS.update({_n + "_ci_s": (3,), _n + "_ci_r": (3,), _n + "_cj_s": (15,), _n + "_cj_r": (15,)})


class Refs:
    pass


def body(*refs):
    ins, outs, rest = refs[:8], refs[8:13], refs[13:]
    m = Refs()
    for name, ref in zip(SCRATCH, rest[: len(SCRATCH)]):
        setattr(m, name, ref)
    for name, ref in zip(SEMS, rest[len(SCRATCH):]):
        setattr(m, name + "_sem", ref)
    dx_hbm, gqs, gos, gqt, got = outs

    dp = lax.axis_index("dp")
    me = lax.axis_index("seq")
    zh, core = dp // 2, lax.rem(dp, 2)
    cx, zl, cy = me // 8, lax.rem(me // 4, 2), lax.rem(me, 4)
    cz = zh * 2 + zl

    def place(x, y, z):
        return ((z // 2) * 2 + core, x * 8 + lax.rem(z, 2) * 4 + y)

    dests = (m.x, None, m.ks, m.kt, m.wqs, m.wos, m.wqt, m.wot)
    loads = [
        None if dst is None else pltpu.make_async_copy(src, dst, m.load_sem.at[i])
        for i, (src, dst) in enumerate(zip(ins, dests))
    ]
    for i in (0, 4, 2, 5, 7, 3, 6):
        loads[i].start()

    barrier = pltpu.get_barrier_semaphore()

    def greet(d, carry):
        pl.semaphore_signal(
            barrier, inc=1, device_id=(dp, lax.rem(me + d, NS)), device_id_type=MESH
        )
        return carry

    lax.fori_loop(1, NS, greet, 0)
    other_core = (zh * 2 + 1 - core, me)
    pl.semaphore_signal(barrier, inc=1, device_id=other_core, device_id_type=MESH)
    far = (1 - zh) * 2 + core
    pl.semaphore_signal(barrier, inc=1, device_id=(far, me), device_id_type=MESH)
    pl.semaphore_signal(
        barrier, inc=1, device_id=(far, cx * 8 + (1 - zl) * 4 + cy), device_id_type=MESH
    )

    def a2a_copy(k, src, dst, d):
        to = lax.rem(me + d, NS)
        return pltpu.make_async_remote_copy(
            src_ref=src.at[to],
            dst_ref=dst.at[me],
            send_sem=m.a2a_s_sem.at[k, d - 1],
            recv_sem=m.a2a_r_sem.at[k, d - 1],
            device_id=(dp, to),
            device_id_type=MESH,
        )

    def a2a_start(k, src, dst):
        def step(d, carry):
            a2a_copy(k, src, dst, d).start()
            return carry

        lax.fori_loop(1, NS, step, 0)

    def a2a_wait(k, src, dst):
        def step(d, carry):
            frm = lax.rem(me + NS - d, NS)
            pltpu.make_async_remote_copy(
                src_ref=src.at[frm],
                dst_ref=dst.at[frm],
                send_sem=m.a2a_s_sem.at[k, d - 1],
                recv_sem=m.a2a_r_sem.at[k, d - 1],
                device_id=(dp, frm),
                device_id_type=MESH,
            ).wait_recv()
            return carry

        lax.fori_loop(1, NS, step, 0)

    def a2a_drain(k, src, dst):
        def step(d, carry):
            a2a_copy(k, src, dst, d).wait_send()
            return carry

        lax.fori_loop(1, NS, step, 0)

    def rows(fn):
        def step(r, carry):
            fn(pl.ds(pl.multiple_of(r * 32, 32), 32), pl.ds(r * 4, 4))
            return carry

        lax.fori_loop(0, 8, step, 0)

    def flat(ref, blk):
        return ref[blk].astype(F32).reshape(32, D)

    def inv_of(zf):
        return lax.rsqrt(jnp.mean(zf * zf, axis=-1, keepdims=True) + 1e-06)

    def normalize(src, dst):
        def fn(r, blk):
            zf = flat(src, blk)
            dst[r, :] = (zf * inv_of(zf)).astype(BF)

        rows(fn)

    def heads(ref, js):
        return jnp.concatenate([ref[j].astype(F32) for j in js], axis=0)

    def qkv_heads(normed, w, hs):
        for n in range(3):
            part = nt(w[INNER * n: INNER * (n + 1), :], normed[...])
            hs[H * n: H * (n + 1)] = part.reshape(H, HD, T).astype(BF)

    def d_proj_mix(dy, keep, wo):
        def fn(r, blk):
            m.dproj[r, :] = (flat(dy, blk) * (flat(keep, blk) * KEEP)).astype(BF)

        rows(fn)
        m.dmh[...] = nt(wo[...], m.dproj[...]).reshape(H, HD, T).astype(BF)

    def softmax(q, k, mask):
        e = jnp.exp(tn(q, k) * SCALE)
        if mask is not None:
            e = jnp.where(mask, e, 0.0)
        return e * (1.0 / jnp.sum(e, axis=-1, keepdims=True))

    def attention_backward(h, p, p_low, q, k, v):
        dm = m.dmh[h]
        dp_ = tn(dm, v)
        ds = (p * (dp_ - jnp.sum(p * dp_, axis=-1, keepdims=True)) * SCALE).astype(BF)
        m.dh[h] = nt(k, ds).astype(BF)
        m.dh[h + 8] = nn(q, ds).astype(BF)
        m.dh[h + 16] = nn(dm, p_low).astype(BF)

    def gather_columns(sec):
        for c in range(2):
            z0 = heads(m.dh, [6 * c + i for i in range(6)])
            z1 = heads(m.dh, [12 + 6 * c + i for i in range(6)])
            parts = [z0[:128], z1[:128], z0[128:], z1[128:]]
            m.dsel[sec, c, 0:864] = jnp.concatenate(parts, axis=0).astype(BF)

    def gather_mixed(sec, mh):
        for c in range(2):
            hs = (2 * c, 2 * c + 1, 4 + 2 * c, 5 + 2 * c)
            m.dsel[sec, c, 864:1152] = heads(mh, hs).astype(BF)

    def input_backward(src, dy, dst, wq):
        m.dqkv[:, 0:1152] = heads(m.dh, range(16)).T.astype(BF)
        m.dqkv[:, 1152:1728] = heads(m.dh, range(16, 24)).T.astype(BF)
        for n in range(3):
            m.dn[:, 384 * n: 384 * (n + 1)] = nn(m.dqkv[...], wq[:, 384 * n: 384 * (n + 1)])

        def fn(r, blk):
            zf = flat(src, blk)
            inv = inv_of(zf)
            c = zf * inv
            dn = m.dn[r, :]
            dz = flat(dy, blk) + inv * (dn - c * jnp.mean(dn * c, axis=-1, keepdims=True))
            dst[blk] = dz.reshape(4, 8, D).astype(BF)

        rows(fn)

    def core_copies(sec):
        pairs = (
            (m.lt.at[sec, 0], m.lt_in.at[sec, 0]),
            (m.lt.at[sec, 1], m.lt_in.at[sec, 1]),
            (m.dsel.at[sec, 1 - core, 0:864], m.dsel_in.at[sec, 0:864]),
            (m.dsel.at[sec, 1 - core, 864:1152], m.dsel_in.at[sec, 864:1152]),
        )
        return [
            pltpu.make_async_remote_copy(
                src_ref=src,
                dst_ref=dst,
                send_sem=m.core_s_sem.at[sec, i],
                recv_sem=m.core_r_sem.at[sec, i],
                device_id=other_core,
                device_id_type=MESH,
            )
            for i, (src, dst) in enumerate(pairs)
        ]

    def transpose_rows(sec, i, src):
        def step(n, carry):
            r = pl.ds(pl.multiple_of(n * 320, 320), 320)
            m.lt[sec, i, r, :] = nt(m.perm[r, :], src[...]).astype(BF)
            return carry

        lax.fori_loop(0, 4, step, 0)

    def grad_of(sec, i, o, lo, hi):
        r = slice(640 * o, 640 * (o + 1))
        acc = nt(m.lt[sec, i, r, :], m.dsel[sec, core, lo:hi, :])
        acc = acc + nt(m.lt_in[sec, i, r, :], m.dsel_in[sec, lo:hi, :])
        return acc

    def widen(acc, width):
        return jnp.concatenate([acc, jnp.zeros((acc.shape[0], width - acc.shape[1]), F32)], axis=1)

    def blocks(acc):
        return acc.reshape(4, 4, RB, acc.shape[1]).astype(BF)

    def grad_first(sec, n):
        dst = getattr(m, n + "_c")
        for o in range(2):
            acc = grad_of(sec, 0, o, 0, 256)
            dst[0, o] = blocks(acc[:, :128])
            dst[1, o] = blocks(acc[:, 128:])

    def grad_rest(sec, n):
        dst = getattr(m, n + "_g")
        for o in range(2):
            acc = grad_of(sec, 0, o, 256, 864)
            if n == "space":
                acc = widen(acc, 640)
            dst[4 * o: 4 * o + 4, :, :, 0: acc.shape[1]] = blocks(acc)

    def grad_out(sec, n):
        dst = getattr(m, n + "_g")
        for o in range(2):
            acc = grad_of(sec, 1, o, 864, 1152)
            if n == "out":
                dst[4 * o: 4 * o + 4] = blocks(widen(acc, 384))
            else:
                dst[4 * o: 4 * o + 4, :, :, 608:896] = blocks(acc)

    def ring(o):
        return cx if o == 0 else cy

    def on_first(o, i):
        return place(i, cy, cz) if o == 0 else place(cx, i, cz)

    def on_second(o, i):
        return place(cx, i, cz) if o == 0 else place(i, cy, cz)

    def remote(src, dst, ssem, rsem, to):
        return pltpu.make_async_remote_copy(
            src_ref=src, dst_ref=dst, send_sem=ssem, recv_sem=rsem, device_id=to, device_id_type=MESH
        )

    class Batch:
        def __init__(self, n):
            self.n = n
            for k in ("g", "r1", "r2", "h", "r3", "z", "r4", "c", "ci", "cs", "cj"):
                setattr(self, k, getattr(m, n + "_" + k, None))
            for k in ("r1", "r2", "r3", "r4", "ci", "cj"):
                for side in "sr":
                    name = k + "_" + side
                    setattr(self, name, getattr(m, n + "_" + name + "_sem", None))

        def first(self, o):
            i = ring(o)
            up, dn, opp = lax.rem(i + 1, 4), lax.rem(i + 3, 4), lax.rem(i + 2, 4)
            one = [
                remote(self.g.at[o * 4 + opp, 2 * k: 2 * k + 2], self.r1.at[o, k],
                       self.r1_s.at[o, k], self.r1_r.at[o, k], on_first(o, to))
                for k, to in ((0, up), (1, dn))
            ]
            two = [
                [
                    remote(self.g.at[o * 4 + to, 2 * b: 2 * b + 2], self.r2.at[o, k, 2 * b: 2 * b + 2],
                           self.r2_s.at[o, k, b], self.r2_r.at[o, k, b], on_first(o, to))
                    for b in range(2)
                ]
                for k, to in ((0, up), (1, dn))
            ]
            return one, two, up, dn, i

        def start(self):
            firsts = [self.first(o) for o in range(2)]
            for one, two, up, dn, i in firsts:
                one[0].start()
                one[1].start()
            for one, two, up, dn, i in firsts:
                two[0][1].start()
                two[1][0].start()

        def relay(self):
            for o in range(2):
                one, two, up, dn, i = self.first(o)
                for side, chunk, b in ((0, up, 0), (1, dn, 1)):
                    one[side].wait_recv()
                    for e in range(2):
                        acc = self.g[o * 4 + chunk, 2 * b + e].astype(F32)
                        acc = acc + self.r1[o, side, e].astype(F32)
                        self.g[o * 4 + chunk, 2 * b + e] = acc.astype(BF)
                    two[side][b].start()

        def second_copies(self, o):
            j = ring(1 - o)
            return [
                remote(self.h.at[o, lax.rem(j + d, 4)], self.r3.at[o, d - 1],
                       self.r3_s.at[o, d - 1], self.r3_r.at[o, d - 1],
                       on_second(o, lax.rem(j + d, 4)))
                for d in (1, 2, 3)
            ]

        def second(self):
            for o in range(2):
                one, two, up, dn, i = self.first(o)
                for side in two:
                    for c in side:
                        c.wait_recv()
                for e in range(4):
                    acc = self.g[o * 4 + i, e].astype(F32)
                    acc = acc + self.r2[o, 0, e].astype(F32)
                    acc = acc + self.r2[o, 1, e].astype(F32)
                    self.h[o, e] = acc.astype(BF)
                for c in self.second_copies(o):
                    c.start()

        def z_copies(self):
            copies = []
            for d in (1, 2, 3):
                z = lax.rem(cz + d, 4)
                copies.append(
                    remote(self.z.at[lax.rem(z, 2), z // 2], self.r4.at[d - 1],
                           self.r4_s.at[d - 1], self.r4_r.at[d - 1], place(cx, cy, z))
                )
            return copies

        def third(self):
            for o in range(2):
                for c in self.second_copies(o):
                    c.wait_recv()
                acc = self.h[o, ring(1 - o)].astype(F32)
                for d in range(3):
                    acc = acc + self.r3[o, d].astype(F32)
                for z in range(2):
                    if self.n == "out":
                        v = acc[:, 144 * z: 144 * (z + 1)]
                    else:
                        v = acc[:, 304 * z: 304 * (z + 1)]
                    if self.n == "time":
                        low = 608 + 144 * z
                        v = jnp.concatenate([v, acc[:, low: low + 144]], axis=1)
                    self.z[o, z] = widen(v, BATCHES[self.n][1]).astype(BF)
            for c in self.z_copies():
                c.start()

        def ci_copies(self):
            copies = []
            for d in (1, 2, 3):
                z = lax.rem(cz + d, 4)
                copies.append(
                    remote(self.c.at[z // 2, lax.rem(z, 2)], self.ci.at[d - 1],
                           self.ci_s.at[d - 1], self.ci_r.at[d - 1], place(cx, cy, z))
                )
            return copies

        def cj_copies(self):
            copies = []
            for d in range(1, 16):
                x, y = lax.rem(cx + d // 4, 4), lax.rem(cy + d % 4, 4)
                a, b = x * (1 - zl) + y * zl, y * (1 - zl) + x * zl
                copies.append(
                    remote(self.cs.at[a, b], self.cj.at[d - 1],
                           self.cj_s.at[d - 1], self.cj_r.at[d - 1], place(x, y, cz))
                )
            return copies

        def c_start(self):
            for c in self.ci_copies():
                c.start()

        def c_second(self):
            for c in self.ci_copies():
                c.wait_recv()

            def add(a, carry):
                acc = self.c[zh, zl, a].astype(F32)
                for d in range(3):
                    acc = acc + self.ci[d, a].astype(F32)
                self.cs[a] = acc.astype(BF)
                return carry

            lax.fori_loop(0, 4, add, 0)
            for c in self.cj_copies():
                c.start()

        def c_end(self):
            for c in self.cj_copies():
                c.wait_recv()
            a, b = cx * (1 - zl) + cy * zl, cy * (1 - zl) + cx * zl
            acc = self.cs[a, b].astype(F32)
            for d in range(15):
                acc = acc + self.cj[d].astype(F32)
            return acc

        def end(self):
            for c in self.z_copies():
                c.wait_recv()
            acc = self.z[zl, zh].astype(F32)
            for d in range(3):
                acc = acc + self.r4[d].astype(F32)
            return acc

        def drain(self):
            for o in range(2):
                one, two, up, dn, i = self.first(o)
                for c in one + two[0] + two[1] + self.second_copies(o):
                    c.wait_send()
            for c in self.z_copies():
                c.wait_send()
            if self.c is not None:
                for c in self.ci_copies() + self.cj_copies():
                    c.wait_send()

    b_time, b_out, b_space = Batch("time"), Batch("out"), Batch("space")

    loads[0].wait()
    normalize(m.x, m.normed_s)
    loads[4].wait()
    qkv_heads(m.normed_s, m.wqs, m.hs_s)
    pl.semaphore_wait(barrier, NS + 2)
    a2a_start(0, ins[1], m.go)
    own = pltpu.make_async_copy(ins[1].at[me], m.go.at[me], m.load_sem.at[1])
    own.start()

    def spatial_head(h, carry):
        p = softmax(m.hs_s[h], m.hs_s[h + 8], None)
        m.probs[h] = p
        m.mh_s[h] = nt(m.hs_s[h + 16], p.astype(BF)).astype(BF)
        return carry

    lax.fori_loop(0, H, spatial_head, 0)
    m.mixed[...] = heads(m.mh_s, range(H)).T.astype(BF)
    loads[2].wait()
    loads[5].wait()
    for n in range(3):
        c = slice(384 * n, 384 * (n + 1))
        proj = nn(m.mixed[...], m.wos[:, c]).reshape(32, 8, 384)
        keep = m.ks[:, :, c].astype(F32) * KEEP
        m.y_out[:, :, c] = (m.x[:, :, c].astype(F32) + proj * keep).astype(BF)
    a2a_start(1, m.y_out, m.y_in)
    m.y_in[me] = m.y_out[me]

    def perm_step(n, carry):
        blocks = []
        for k in (2 * n, 2 * n + 1):
            o, a, b = k // 16, lax.rem(k // 4, 4), lax.rem(k, 4)
            x = a * (1 - o) + b * o
            y = b * (1 - o) + a * o
            s = x * 8 + o * 4 + y
            row = lax.broadcasted_iota(jnp.int32, (RB, D), 0)
            col = lax.broadcasted_iota(jnp.int32, (RB, D), 1)
            hit = (col == row + 36 * s) & (row < 36)
            blocks.append(jnp.where(hit, 1.0, 0.0))
        both = jnp.concatenate(blocks, axis=0).astype(BF)
        m.perm[pl.ds(pl.multiple_of(n * 80, 80), 80), :] = both
        return carry

    lax.fori_loop(0, NS // 2, perm_step, 0)
    gather_mixed(1, m.mh_s)
    core_copies(1)[3].start()

    own.wait()
    a2a_wait(0, m.go, m.go)
    loads[3].wait()
    loads[7].wait()
    d_proj_mix(m.go, m.kt, m.wot)
    transpose_rows(0, 1, m.dproj)
    core_copies(0)[1].start()
    transpose_rows(1, 0, m.normed_s)
    core_copies(1)[0].start()
    a2a_wait(1, m.y_out, m.y_in)
    normalize(m.y_in, m.normed_t)
    loads[6].wait()
    qkv_heads(m.normed_t, m.wqt, m.hs_t)

    def temporal_head(h, carry):
        i = lax.broadcasted_iota(jnp.int32, (T, T), 0)
        j = lax.broadcasted_iota(jnp.int32, (T, T), 1)
        mask = ((i - j) & 7) == 0
        q, k, v = m.hs_t[h], m.hs_t[h + 8], m.hs_t[h + 16]
        p = softmax(q, k, mask)
        p_low = p.astype(BF)
        m.mh_t[h] = nt(v, p_low).astype(BF)
        attention_backward(h, p, p_low, q, k, v)
        return carry

    lax.fori_loop(0, H, temporal_head, 0)
    input_backward(m.y_in, m.go, m.d_out, m.wqt)
    a2a_start(2, m.d_out, m.d_in)
    m.d_in[me] = m.d_out[me]
    gather_columns(0)
    gather_mixed(0, m.mh_t)
    core_copies(0)[2].start()
    core_copies(0)[3].start()
    transpose_rows(0, 0, m.normed_t)
    core_copies(0)[0].start()
    for c in core_copies(0):
        c.wait_recv()
    grad_first(0, "time")
    b_time.c_start()
    grad_rest(0, "time")
    grad_out(0, "time")
    b_time.start()

    a2a_wait(2, m.d_out, m.d_in)
    d_proj_mix(m.d_in, m.ks, m.wos)
    transpose_rows(1, 1, m.dproj)
    core_copies(1)[1].start()
    b_time.relay()

    def spatial_back(h, carry):
        p = m.probs[h]
        attention_backward(h, p, p.astype(BF), m.hs_s[h], m.hs_s[h + 8], m.hs_s[h + 16])
        return carry

    lax.fori_loop(0, H, spatial_back, 0)
    gather_columns(1)
    core_copies(1)[2].start()
    core_copies(1)[1].wait_recv()
    core_copies(1)[3].wait_recv()
    grad_out(1, "out")
    b_out.start()
    core_copies(1)[0].wait_recv()
    core_copies(1)[2].wait_recv()
    grad_first(1, "space")
    b_space.c_start()
    grad_rest(1, "space")
    b_space.start()
    b_time.second()
    b_time.c_second()
    b_out.relay()
    input_backward(m.x, m.d_in, m.dx, m.wqs)
    store = pltpu.make_async_copy(m.dx, dx_hbm, m.store_sem.at[0])
    store.start()
    b_space.relay()
    b_space.c_second()
    b_time.third()
    b_out.second()
    b_space.second()
    first = b_time.c_end()
    rest = b_time.end()
    gqt[...] = jnp.concatenate([first[0:36], rest[0:36, 0:304]], axis=1)
    got[...] = rest[0:36, 304:448]
    b_out.third()
    b_space.third()
    first = b_space.c_end()
    gos[...] = b_out.end()[0:36, 0:144]
    rest = b_space.end()
    gqs[...] = jnp.concatenate([first[0:36], rest[0:36, 0:304]], axis=1)

    a2a_drain(0, ins[1], m.go)
    a2a_drain(1, m.y_out, m.y_in)
    a2a_drain(2, m.d_out, m.d_in)
    for c in core_copies(0) + core_copies(1):
        c.wait_send()
    b_time.drain()
    b_out.drain()
    b_space.drain()
    store.wait()


def hand_over(*refs):
    sem = refs[10]
    copies = [pltpu.make_async_copy(refs[i], refs[5 + i], sem.at[i]) for i in range(5)]
    for c in copies:
        c.start()
    for c in copies:
        c.wait()


def shards(
    block_input,
    out_grad,
    spatial_keep,
    temporal_keep,
    spatial_qkv,
    spatial_out,
    temporal_qkv,
    temporal_out,
):
    hbm = pl.BlockSpec(memory_space=pl.ANY)
    vmem = pl.BlockSpec(memory_space=pltpu.VMEM)
    outs = pl.pallas_call(
        body,
        out_shape=(
            jax.ShapeDtypeStruct((32, 8, D), BF),
            jax.ShapeDtypeStruct((36, 432), F32),
            jax.ShapeDtypeStruct((36, 144), F32),
            jax.ShapeDtypeStruct((36, 432), F32),
            jax.ShapeDtypeStruct((36, 144), F32),
        ),
        in_specs=[hbm] * 8,
        out_specs=(hbm, vmem, vmem, vmem, vmem),
        scratch_shapes=[pltpu.VMEM(s, d) for s, d in SCRATCH.values()]
        + [pltpu.SemaphoreType.DMA(s) for s in SEMS.values()],
        compiler_params=pltpu.CompilerParams(
            collective_id=0, has_side_effects=True, vmem_limit_bytes=63 * 2**20
        ),
    )(
        block_input.reshape(32, 8, D),
        out_grad.reshape(32, 8, D),
        spatial_keep.reshape(32, 8, D),
        temporal_keep.reshape(32, 8, D),
        spatial_qkv.T,
        spatial_out.T,
        temporal_qkv.T,
        temporal_out.T,
    )
    outs = pl.pallas_call(
        hand_over,
        out_shape=tuple(jax.ShapeDtypeStruct(o.shape, o.dtype) for o in outs),
        in_specs=[vmem] * 5,
        out_specs=(hbm,) * 5,
        scratch_shapes=[pltpu.SemaphoreType.DMA((5,))],
    )(*outs)
    return (outs[0].reshape(1, 1, T, D),) + tuple(outs[1:])


def solution(mesh):
    return jax.shard_map(
        shards,
        mesh=mesh,
        in_specs=(
            P("dp", "seq", None, None),
            P("dp", "seq", None, None),
            P("dp", "seq", None, None),
            P("dp", None, "seq", None),
            P(),
            P(),
            P(),
            P(),
        ),
        out_specs=(
            P("dp", "seq", None, None),
            P("seq", "dp"),
            P("seq", "dp"),
            P("seq", "dp"),
            P("seq", "dp"),
        ),
        check_vma=False,
    )
```

```python
import jax
import jax.numpy as jnp
from jax import lax
from jax.experimental import pallas as pl
from jax.experimental.pallas import tpu as pltpu
from jax.sharding import PartitionSpec as P

D = 1152
H = 8
HD = 72
INNER = 576
T = 256
NS = 32
RB = 40
PB = 72
HEADS_AT_ONCE = 4
MESH = pl.DeviceIdType.MESH
BF = jnp.bfloat16
F32 = jnp.float32
SCALE = HD ** (-0.5)
KEEP = 1.0 / 0.9


def nt(a, b):
    return lax.dot_general(a, b, (((1,), (1,)), ((), ())), preferred_element_type=F32)


def tn(a, b):
    return lax.dot_general(a, b, (((0,), (0,)), ((), ())), preferred_element_type=F32)


def nn(a, b):
    return jnp.dot(a, b, preferred_element_type=F32)


SCRATCH = dict(
    x=((32, 8, D), BF),
    ks=((32, 8, D), jnp.int32),
    kt=((32, 8, D), jnp.int32),
    wqs=((3 * INNER, D), BF),
    wos=((INNER, D), BF),
    wqt=((3 * INNER, D), BF),
    wot=((INNER, D), BF),
    go=((NS, 8, D), BF),
    y_out=((NS, 8, D), BF),
    y_in=((NS, 8, D), BF),
    d_out=((NS, 8, D), BF),
    d_in=((NS, 8, D), BF),
    normed_s=((T, D), BF),
    normed_t=((T, D), BF),
    hs_s=((24, HD, T), BF),
    hs_t=((24, HD, T), BF),
    probs=((H, T, T), F32),
    mh_s=((H, HD, T), BF),
    mh_t=((H, HD, T), BF),
    mixed=((T, INNER), BF),
    dproj=((T, D), BF),
    dmh=((H, HD, T), BF),
    dh=((24, HD, T), BF),
    dqkv=((T, 3 * INNER), BF),
    dn=((T, D), F32),
    dsel=((2, 2, D, T), BF),
    dsel_in=((2, D, T), BF),
    perm=((D, D), BF),
    lt=((2, 2, D, T), BF),
    lt_in=((2, 2, D, T), BF),
    dx=((32, 8, D), BF),
)
SEMS = dict(
    load=(8,),
    store=(1,),
    a2a_s=(3, 31),
    a2a_r=(3, 31),
    core_s=(2, 4),
    core_r=(2, 4),
)
BATCHES = dict(time=(896, 512, True), out=(384, 256, False), space=(640, 384, True))
for _n, (_w, _z, _c) in BATCHES.items():
    SCRATCH.update({
        _n + "_g": ((8, 2, PB, _w), BF),
        _n + "_r1": ((2, 2, PB, _w), BF),
        _n + "_r2": ((2, 2, 2, PB, _w), BF),
        _n + "_h": ((2, 4, RB, _w), BF),
        _n + "_r3": ((2, 3, RB, _w), BF),
        _n + "_z": ((2, 2, RB, _z), BF),
        _n + "_r4": ((3, RB, _z), BF),
    })
    SEMS.update({
        _n + "_r1_s": (2, 2), _n + "_r1_r": (2, 2), _n + "_r2_s": (2, 2, 2), _n + "_r2_r": (2, 2, 2),
        _n + "_r3_s": (2, 3), _n + "_r3_r": (2, 3), _n + "_r4_s": (3,), _n + "_r4_r": (3,),
    })
    if _c:
        SCRATCH.update({
            _n + "_c": ((2, 2, 4, 2, PB, 128), BF),
            _n + "_ci": ((3, 4, 2, PB, 128), BF),
            _n + "_cs": ((4, 4, RB, 128), BF),
            _n + "_cj": ((15, RB, 128), BF),
        })
        SEMS.update({_n + "_ci_s": (3,), _n + "_ci_r": (3,), _n + "_cj_s": (15,), _n + "_cj_r": (15,)})


class Refs:
    pass


def body(*refs):
    ins, outs, rest = refs[:8], refs[8:13], refs[13:]
    m = Refs()
    for name, ref in zip(SCRATCH, rest[: len(SCRATCH)]):
        setattr(m, name, ref)
    for name, ref in zip(SEMS, rest[len(SCRATCH):]):
        setattr(m, name + "_sem", ref)
    dx_hbm, gqs, gos, gqt, got = outs

    dp = lax.axis_index("dp")
    me = lax.axis_index("seq")
    zh, core = dp // 2, lax.rem(dp, 2)
    cx, zl, cy = me // 8, lax.rem(me // 4, 2), lax.rem(me, 4)
    cz = zh * 2 + zl

    def place(x, y, z):
        return ((z // 2) * 2 + core, x * 8 + lax.rem(z, 2) * 4 + y)

    dests = (m.x, None, m.ks, m.kt, m.wqs, m.wos, m.wqt, m.wot)
    loads = [
        None if dst is None else pltpu.make_async_copy(src, dst, m.load_sem.at[i])
        for i, (src, dst) in enumerate(zip(ins, dests))
    ]
    loads[0].start()
    loads[4].start()

    barrier = pltpu.get_barrier_semaphore()

    def greet(d, carry):
        pl.semaphore_signal(
            barrier, inc=1, device_id=(dp, lax.rem(me + d, NS)), device_id_type=MESH
        )
        return carry

    lax.fori_loop(1, NS, greet, 0)
    other_core = (zh * 2 + 1 - core, me)
    pl.semaphore_signal(barrier, inc=1, device_id=other_core, device_id_type=MESH)
    far = (1 - zh) * 2 + core
    pl.semaphore_signal(barrier, inc=1, device_id=(far, me), device_id_type=MESH)
    pl.semaphore_signal(
        barrier, inc=1, device_id=(far, cx * 8 + (1 - zl) * 4 + cy), device_id_type=MESH
    )

    def a2a_copy(k, src, dst, d):
        to = lax.rem(me + d, NS)
        return pltpu.make_async_remote_copy(
            src_ref=src.at[to],
            dst_ref=dst.at[me],
            send_sem=m.a2a_s_sem.at[k, d - 1],
            recv_sem=m.a2a_r_sem.at[k, d - 1],
            device_id=(dp, to),
            device_id_type=MESH,
        )

    def a2a_start(k, src, dst):
        def step(d, carry):
            a2a_copy(k, src, dst, d).start()
            return carry

        lax.fori_loop(1, NS, step, 0)

    def a2a_send(k, src, dst, to):
        d = lax.rem(to - me + NS, NS)

        @pl.when(d != 0)
        def _():
            a2a_copy(k, src, dst, d).start()

    def a2a_wait(k, src, dst):
        def step(d, carry):
            frm = lax.rem(me + NS - d, NS)
            pltpu.make_async_remote_copy(
                src_ref=src.at[frm],
                dst_ref=dst.at[frm],
                send_sem=m.a2a_s_sem.at[k, d - 1],
                recv_sem=m.a2a_r_sem.at[k, d - 1],
                device_id=(dp, frm),
                device_id_type=MESH,
            ).wait_recv()
            return carry

        lax.fori_loop(1, NS, step, 0)

    def a2a_drain(k, src, dst):
        def step(d, carry):
            a2a_copy(k, src, dst, d).wait_send()
            return carry

        lax.fori_loop(1, NS, step, 0)

    def rows(fn, first=0, then=None):
        def step(i, carry):
            r = lax.rem(i + first, 8)
            fn(pl.ds(pl.multiple_of(r * 32, 32), 32), pl.ds(r * 4, 4))
            if then is not None:
                then(r)
            return carry

        lax.fori_loop(0, 8, step, 0)

    def flat(ref, blk):
        return ref[blk].astype(F32).reshape(32, D)

    def inv_of(zf):
        return lax.rsqrt(jnp.mean(zf * zf, axis=-1, keepdims=True) + 1e-06)

    def normalize(src, dst):
        def fn(r, blk):
            zf = flat(src, blk)
            dst[r, :] = (zf * inv_of(zf)).astype(BF)

        rows(fn)

    def heads(ref, js):
        return jnp.concatenate([ref[j].astype(F32) for j in js], axis=0)

    def qkv_heads(normed, w, hs):
        for n in range(3):
            part = nt(w[INNER * n: INNER * (n + 1), :], normed[...])
            hs[H * n: H * (n + 1)] = part.reshape(H, HD, T).astype(BF)

    def d_proj_mix(dy, keep, wo):
        def fn(r, blk):
            m.dproj[r, :] = (flat(dy, blk) * (flat(keep, blk) * KEEP)).astype(BF)

        rows(fn)
        m.dmh[...] = nt(wo[...], m.dproj[...]).reshape(H, HD, T).astype(BF)

    def some_heads(lo, hi, fn):
        def step(i, carry):
            for j in range(HEADS_AT_ONCE):
                fn(i * HEADS_AT_ONCE + j)
            return carry

        lax.fori_loop(lo // HEADS_AT_ONCE, hi // HEADS_AT_ONCE, step, 0)

    def softmax(q, k, mask):
        e = jnp.exp(tn(q, k) * SCALE)
        if mask is not None:
            e = jnp.where(mask, e, 0.0)
        return e * (1.0 / jnp.sum(e, axis=-1, keepdims=True))

    def attention_backward(h, p, p_low, q, k, v):
        dm = m.dmh[h]
        dp_ = tn(dm, v)
        ds = (p * (dp_ - jnp.sum(p * dp_, axis=-1, keepdims=True)) * SCALE).astype(BF)
        m.dh[h] = nt(k, ds).astype(BF)
        m.dh[h + 8] = nn(q, ds).astype(BF)
        m.dh[h + 16] = nn(dm, p_low).astype(BF)

    def gather_columns(sec):
        for c in range(2):
            z0 = heads(m.dh, [6 * c + i for i in range(6)])
            z1 = heads(m.dh, [12 + 6 * c + i for i in range(6)])
            parts = [z0[:128], z1[:128], z0[128:], z1[128:]]
            m.dsel[sec, c, 0:864] = jnp.concatenate(parts, axis=0).astype(BF)

    def gather_mixed(sec, mh):
        for c in range(2):
            hs = (2 * c, 2 * c + 1, 4 + 2 * c, 5 + 2 * c)
            m.dsel[sec, c, 864:1152] = heads(mh, hs).astype(BF)

    def input_backward(src, dy, dst, wq, then=None):
        m.dqkv[:, 0:1152] = heads(m.dh, range(16)).T.astype(BF)
        m.dqkv[:, 1152:1728] = heads(m.dh, range(16, 24)).T.astype(BF)
        for n in range(3):
            m.dn[:, 384 * n: 384 * (n + 1)] = nn(m.dqkv[...], wq[:, 384 * n: 384 * (n + 1)])

        def fn(r, blk):
            zf = flat(src, blk)
            inv = inv_of(zf)
            c = zf * inv
            dn = m.dn[r, :]
            dz = flat(dy, blk) + inv * (dn - c * jnp.mean(dn * c, axis=-1, keepdims=True))
            dst[blk] = dz.reshape(4, 8, D).astype(BF)

        rows(fn, me // 4, then)

    def core_copies(sec):
        pairs = (
            (m.lt.at[sec, 0], m.lt_in.at[sec, 0]),
            (m.lt.at[sec, 1], m.lt_in.at[sec, 1]),
            (m.dsel.at[sec, 1 - core, 0:864], m.dsel_in.at[sec, 0:864]),
            (m.dsel.at[sec, 1 - core, 864:1152], m.dsel_in.at[sec, 864:1152]),
        )
        return [
            pltpu.make_async_remote_copy(
                src_ref=src,
                dst_ref=dst,
                send_sem=m.core_s_sem.at[sec, i],
                recv_sem=m.core_r_sem.at[sec, i],
                device_id=other_core,
                device_id_type=MESH,
            )
            for i, (src, dst) in enumerate(pairs)
        ]

    def transpose_rows(sec, i, src):
        def step(n, carry):
            r = pl.ds(pl.multiple_of(n * 288, 288), 288)
            m.lt[sec, i, r, :] = nt(m.perm[r, :], src[...]).astype(BF)
            return carry

        lax.fori_loop(0, 4, step, 0)

    def grad_of(sec, i, o, lo, hi):
        r = slice(576 * o, 576 * (o + 1))
        acc = nt(m.lt[sec, i, r, :], m.dsel[sec, core, lo:hi, :])
        acc = acc + nt(m.lt_in[sec, i, r, :], m.dsel_in[sec, lo:hi, :])
        return acc

    def widen(acc, width):
        return jnp.concatenate([acc, jnp.zeros((acc.shape[0], width - acc.shape[1]), F32)], axis=1)

    def lower(acc):
        return jnp.concatenate([acc[36:72], jnp.zeros((4, acc.shape[1]), F32)], axis=0).astype(BF)

    def blocks(acc):
        return acc.reshape(4, 2, PB, acc.shape[1]).astype(BF)

    def grad_first(sec, n):
        dst = getattr(m, n + "_c")
        for o in range(2):
            acc = grad_of(sec, 0, o, 0, 256)
            dst[0, o] = blocks(acc[:, :128])
            dst[1, o] = blocks(acc[:, 128:])

    def grad_rest(sec, n):
        dst = getattr(m, n + "_g")
        for o in range(2):
            acc = grad_of(sec, 0, o, 256, 864)
            if n == "space":
                acc = widen(acc, 640)
            dst[4 * o: 4 * o + 4, :, :, 0: acc.shape[1]] = blocks(acc)

    def grad_out(sec, n):
        dst = getattr(m, n + "_g")
        for o in range(2):
            acc = grad_of(sec, 1, o, 864, 1152)
            if n == "out":
                dst[4 * o: 4 * o + 4] = blocks(widen(acc, 384))
            else:
                dst[4 * o: 4 * o + 4, :, :, 608:896] = blocks(acc)

    def ring(o):
        return cx if o == 0 else cy

    def on_first(o, i):
        return place(i, cy, cz) if o == 0 else place(cx, i, cz)

    def on_second(o, i):
        return place(cx, i, cz) if o == 0 else place(i, cy, cz)

    def remote(src, dst, ssem, rsem, to):
        return pltpu.make_async_remote_copy(
            src_ref=src, dst_ref=dst, send_sem=ssem, recv_sem=rsem, device_id=to, device_id_type=MESH
        )

    class Batch:
        def __init__(self, n):
            self.n = n
            for k in ("g", "r1", "r2", "h", "r3", "z", "r4", "c", "ci", "cs", "cj"):
                setattr(self, k, getattr(m, n + "_" + k, None))
            for k in ("r1", "r2", "r3", "r4", "ci", "cj"):
                for side in "sr":
                    name = k + "_" + side
                    setattr(self, name, getattr(m, n + "_" + name + "_sem", None))

        def first(self, o):
            i = ring(o)
            up, dn, opp = lax.rem(i + 1, 4), lax.rem(i + 3, 4), lax.rem(i + 2, 4)
            one = [
                remote(self.g.at[o * 4 + opp, k], self.r1.at[o, k],
                       self.r1_s.at[o, k], self.r1_r.at[o, k], on_first(o, to))
                for k, to in ((0, up), (1, dn))
            ]
            two = [
                [
                    remote(self.g.at[o * 4 + to, b], self.r2.at[o, k, b],
                           self.r2_s.at[o, k, b], self.r2_r.at[o, k, b], on_first(o, to))
                    for b in range(2)
                ]
                for k, to in ((0, up), (1, dn))
            ]
            return one, two, up, dn, i

        def start(self):
            firsts = [self.first(o) for o in range(2)]
            for one, two, up, dn, i in firsts:
                one[0].start()
                one[1].start()
            for one, two, up, dn, i in firsts:
                two[0][1].start()
                two[1][0].start()

        def relay(self):
            for o in range(2):
                one, two, up, dn, i = self.first(o)
                for side, chunk, b in ((0, up, 0), (1, dn, 1)):
                    one[side].wait_recv()
                    acc = self.g[o * 4 + chunk, b].astype(F32)
                    acc = acc + self.r1[o, side].astype(F32)
                    self.g[o * 4 + chunk, b] = acc.astype(BF)
                    two[side][b].start()

        def second_copies(self, o):
            j = ring(1 - o)
            return [
                remote(self.h.at[o, lax.rem(j + d, 4)], self.r3.at[o, d - 1],
                       self.r3_s.at[o, d - 1], self.r3_r.at[o, d - 1],
                       on_second(o, lax.rem(j + d, 4)))
                for d in (1, 2, 3)
            ]

        def second(self):
            for o in range(2):
                one, two, up, dn, i = self.first(o)
                for side in two:
                    for c in side:
                        c.wait_recv()
                for e in range(2):
                    acc = self.g[o * 4 + i, e].astype(F32)
                    acc = acc + self.r2[o, 0, e].astype(F32)
                    acc = acc + self.r2[o, 1, e].astype(F32)
                    self.h[o, 2 * e] = acc[0:40].astype(BF)
                    self.h[o, 2 * e + 1] = lower(acc)
                for c in self.second_copies(o):
                    c.start()

        def z_copies(self):
            copies = []
            for d in (1, 2, 3):
                z = lax.rem(cz + d, 4)
                copies.append(
                    remote(self.z.at[lax.rem(z, 2), z // 2], self.r4.at[d - 1],
                           self.r4_s.at[d - 1], self.r4_r.at[d - 1], place(cx, cy, z))
                )
            return copies

        def third(self):
            for o in range(2):
                for c in self.second_copies(o):
                    c.wait_recv()
                acc = self.h[o, ring(1 - o)].astype(F32)
                for d in range(3):
                    acc = acc + self.r3[o, d].astype(F32)
                for z in range(2):
                    if self.n == "out":
                        v = acc[:, 144 * z: 144 * (z + 1)]
                    else:
                        v = acc[:, 304 * z: 304 * (z + 1)]
                    if self.n == "time":
                        low = 608 + 144 * z
                        v = jnp.concatenate([v, acc[:, low: low + 144]], axis=1)
                    self.z[o, z] = widen(v, BATCHES[self.n][1]).astype(BF)
            for c in self.z_copies():
                c.start()

        def ci_copies(self):
            copies = []
            for d in (1, 2, 3):
                z = lax.rem(cz + d, 4)
                copies.append(
                    remote(self.c.at[z // 2, lax.rem(z, 2)], self.ci.at[d - 1],
                           self.ci_s.at[d - 1], self.ci_r.at[d - 1], place(cx, cy, z))
                )
            return copies

        def cj_copies(self):
            copies = []
            for d in range(1, 16):
                x, y = lax.rem(cx + d // 4, 4), lax.rem(cy + d % 4, 4)
                a, b = x * (1 - zl) + y * zl, y * (1 - zl) + x * zl
                copies.append(
                    remote(self.cs.at[a, b], self.cj.at[d - 1],
                           self.cj_s.at[d - 1], self.cj_r.at[d - 1], place(x, y, cz))
                )
            return copies

        def c_start(self):
            for c in self.ci_copies():
                c.start()

        def c_second(self):
            for c in self.ci_copies():
                c.wait_recv()

            def add(a, carry):
                for e in range(2):
                    acc = self.c[zh, zl, a, e].astype(F32)
                    for d in range(3):
                        acc = acc + self.ci[d, a, e].astype(F32)
                    self.cs[a, 2 * e] = acc[0:40].astype(BF)
                    self.cs[a, 2 * e + 1] = lower(acc)
                return carry

            lax.fori_loop(0, 4, add, 0)
            for c in self.cj_copies():
                c.start()

        def c_end(self):
            for c in self.cj_copies():
                c.wait_recv()
            a, b = cx * (1 - zl) + cy * zl, cy * (1 - zl) + cx * zl
            acc = self.cs[a, b].astype(F32)
            for d in range(15):
                acc = acc + self.cj[d].astype(F32)
            return acc

        def end(self):
            for c in self.z_copies():
                c.wait_recv()
            acc = self.z[zl, zh].astype(F32)
            for d in range(3):
                acc = acc + self.r4[d].astype(F32)
            return acc

        def drain(self):
            for o in range(2):
                one, two, up, dn, i = self.first(o)
                for c in one + two[0] + two[1] + self.second_copies(o):
                    c.wait_send()
            for c in self.z_copies():
                c.wait_send()
            if self.c is not None:
                for c in self.ci_copies() + self.cj_copies():
                    c.wait_send()

    b_time, b_out, b_space = Batch("time"), Batch("out"), Batch("space")

    loads[0].wait()
    normalize(m.x, m.normed_s)
    pl.semaphore_wait(barrier, NS + 2)
    a2a_start(0, ins[1], m.go)
    own = pltpu.make_async_copy(ins[1].at[me], m.go.at[me], m.load_sem.at[1])
    own.start()
    loads[4].wait()
    for i in (5, 2, 7, 3, 6):
        loads[i].start()
    qkv_heads(m.normed_s, m.wqs, m.hs_s)

    loads[2].wait()
    loads[5].wait()
    for half in range(2):
        q_part, f_part = slice(128 * half, 128 * (half + 1)), slice(16 * half, 16 * (half + 1))

        def spatial_head(h):
            p = softmax(m.hs_s[h, :, q_part], m.hs_s[h + 8], None)
            m.probs[h, q_part, :] = p
            m.mh_s[h, :, q_part] = nt(m.hs_s[h + 16], p.astype(BF)).astype(BF)

        some_heads(0, H, spatial_head)
        part = jnp.concatenate([m.mh_s[h, :, q_part].astype(F32) for h in range(H)], axis=0)
        m.mixed[q_part, :] = part.T.astype(BF)
        for n in range(3):
            c = slice(384 * n, 384 * (n + 1))
            proj = nn(m.mixed[q_part, :], m.wos[:, c]).reshape(16, 8, 384)
            keep = m.ks[f_part, :, c].astype(F32) * KEEP
            m.y_out[f_part, :, c] = (m.x[f_part, :, c].astype(F32) + proj * keep).astype(BF)

        def send_part(i, carry):
            a2a_send(1, m.y_out, m.y_in, 16 * half + lax.rem(me + i, 16))
            return carry

        lax.fori_loop(0, 16, send_part, 0)
    m.y_in[me] = m.y_out[me]

    def perm_step(n, carry):
        o, a = n // 4, lax.rem(n, 4)
        row = lax.broadcasted_iota(jnp.int32, (PB, D), 0)
        col = lax.broadcasted_iota(jnp.int32, (PB, D), 1)
        pairs = []
        for b in (0, 2):
            s0 = (a * (1 - o) + b * o) * 8 + o * 4 + b * (1 - o) + a * o
            s1 = s0 + 8 * o + 1 - o
            target = jnp.where(row < 36, row + 36 * s0, row + 36 * s1 - 36)
            pairs.append(jnp.where(col == target, 1.0, 0.0))
        both = jnp.concatenate(pairs, axis=0).astype(BF)
        m.perm[pl.ds(pl.multiple_of(n * 144, 144), 144), :] = both
        return carry

    lax.fori_loop(0, 8, perm_step, 0)
    gather_mixed(1, m.mh_s)
    core_copies(1)[3].start()

    own.wait()
    a2a_wait(0, m.go, m.go)
    loads[3].wait()
    loads[7].wait()
    d_proj_mix(m.go, m.kt, m.wot)
    transpose_rows(0, 1, m.dproj)
    core_copies(0)[1].start()
    transpose_rows(1, 0, m.normed_s)
    core_copies(1)[0].start()
    a2a_wait(1, m.y_out, m.y_in)
    normalize(m.y_in, m.normed_t)
    loads[6].wait()
    qkv_heads(m.normed_t, m.wqt, m.hs_t)

    def temporal_head(h):
        i = lax.broadcasted_iota(jnp.int32, (T, T), 0)
        j = lax.broadcasted_iota(jnp.int32, (T, T), 1)
        mask = ((i - j) & 7) == 0
        q, k, v = m.hs_t[h], m.hs_t[h + 8], m.hs_t[h + 16]
        p = softmax(q, k, mask)
        p_low = p.astype(BF)
        m.mh_t[h] = nt(v, p_low).astype(BF)
        attention_backward(h, p, p_low, q, k, v)

    some_heads(0, H, temporal_head)
    def send_rows(r):
        for j in range(4):
            a2a_send(2, m.d_out, m.d_in, r * 4 + lax.rem(me + j, 4))

    input_backward(m.y_in, m.go, m.d_out, m.wqt, send_rows)
    m.d_in[me] = m.d_out[me]
    gather_columns(0)
    gather_mixed(0, m.mh_t)
    core_copies(0)[2].start()
    core_copies(0)[3].start()
    transpose_rows(0, 0, m.normed_t)
    core_copies(0)[0].start()
    for c in core_copies(0):
        c.wait_recv()
    grad_first(0, "time")
    b_time.c_start()
    grad_rest(0, "time")
    grad_out(0, "time")
    b_time.start()

    a2a_wait(2, m.d_out, m.d_in)
    d_proj_mix(m.d_in, m.ks, m.wos)
    transpose_rows(1, 1, m.dproj)
    core_copies(1)[1].start()

    def spatial_back(h):
        p = m.probs[h]
        attention_backward(h, p, p.astype(BF), m.hs_s[h], m.hs_s[h + 8], m.hs_s[h + 16])

    some_heads(0, H // 2, spatial_back)
    b_time.relay()
    core_copies(1)[1].wait_recv()
    core_copies(1)[3].wait_recv()
    grad_out(1, "out")
    b_out.start()
    some_heads(H // 2, H, spatial_back)
    gather_columns(1)
    core_copies(1)[2].start()
    b_time.c_second()
    b_time.second()
    core_copies(1)[0].wait_recv()
    core_copies(1)[2].wait_recv()
    grad_first(1, "space")
    b_space.c_start()
    grad_rest(1, "space")
    b_space.start()
    b_out.relay()
    b_time.third()
    input_backward(m.x, m.d_in, m.dx, m.wqs)
    store = pltpu.make_async_copy(m.dx, dx_hbm, m.store_sem.at[0])
    store.start()
    b_space.relay()
    b_out.second()
    first = b_time.c_end()
    rest = b_time.end()
    gqt[...] = jnp.concatenate([first[0:36], rest[0:36, 0:304]], axis=1)
    got[...] = rest[0:36, 304:448]
    b_space.c_second()
    b_out.third()
    b_space.second()
    b_space.third()
    first = b_space.c_end()
    gos[...] = b_out.end()[0:36, 0:144]
    rest = b_space.end()
    gqs[...] = jnp.concatenate([first[0:36], rest[0:36, 0:304]], axis=1)

    a2a_drain(0, ins[1], m.go)
    a2a_drain(1, m.y_out, m.y_in)
    a2a_drain(2, m.d_out, m.d_in)
    for c in core_copies(0) + core_copies(1):
        c.wait_send()
    b_time.drain()
    b_out.drain()
    b_space.drain()
    store.wait()


def hand_over(*refs):
    sem = refs[10]
    copies = [pltpu.make_async_copy(refs[i], refs[5 + i], sem.at[i]) for i in range(5)]
    for c in copies:
        c.start()
    for c in copies:
        c.wait()


def shards(
    block_input,
    out_grad,
    spatial_keep,
    temporal_keep,
    spatial_qkv,
    spatial_out,
    temporal_qkv,
    temporal_out,
):
    hbm = pl.BlockSpec(memory_space=pl.ANY)
    vmem = pl.BlockSpec(memory_space=pltpu.VMEM)
    outs = pl.pallas_call(
        body,
        out_shape=(
            jax.ShapeDtypeStruct((32, 8, D), BF),
            jax.ShapeDtypeStruct((36, 432), F32),
            jax.ShapeDtypeStruct((36, 144), F32),
            jax.ShapeDtypeStruct((36, 432), F32),
            jax.ShapeDtypeStruct((36, 144), F32),
        ),
        in_specs=[hbm] * 8,
        out_specs=(hbm, vmem, vmem, vmem, vmem),
        scratch_shapes=[pltpu.VMEM(s, d) for s, d in SCRATCH.values()]
        + [pltpu.SemaphoreType.DMA(s) for s in SEMS.values()],
        compiler_params=pltpu.CompilerParams(
            collective_id=0, has_side_effects=True, vmem_limit_bytes=63 * 2**20
        ),
    )(
        block_input.reshape(32, 8, D),
        out_grad.reshape(32, 8, D),
        spatial_keep.reshape(32, 8, D),
        temporal_keep.reshape(32, 8, D),
        spatial_qkv.T,
        spatial_out.T,
        temporal_qkv.T,
        temporal_out.T,
    )
    outs = pl.pallas_call(
        hand_over,
        out_shape=tuple(jax.ShapeDtypeStruct(o.shape, o.dtype) for o in outs),
        in_specs=[vmem] * 5,
        out_specs=(hbm,) * 5,
        scratch_shapes=[pltpu.SemaphoreType.DMA((5,))],
    )(*outs)
    return (outs[0].reshape(1, 1, T, D),) + tuple(outs[1:])


def solution(mesh):
    return jax.shard_map(
        shards,
        mesh=mesh,
        in_specs=(
            P("dp", "seq", None, None),
            P("dp", "seq", None, None),
            P("dp", "seq", None, None),
            P("dp", None, "seq", None),
            P(),
            P(),
            P(),
            P(),
        ),
        out_specs=(
            P("dp", "seq", None, None),
            P("seq", "dp"),
            P("seq", "dp"),
            P("seq", "dp"),
            P("seq", "dp"),
        ),
        check_vma=False,
    )
```

```python
import jax
import jax.numpy as jnp
from jax import lax
from jax.experimental import pallas as pl
from jax.experimental.pallas import tpu as pltpu
from jax.sharding import PartitionSpec as P

D = 1152
H = 8
HD = 72
INNER = 576
T = 256
NS = 32
RB = 40
PB = 72
HEADS_AT_ONCE = 4
MESH = pl.DeviceIdType.MESH
BF = jnp.bfloat16
F32 = jnp.float32
SCALE = HD ** (-0.5)
KEEP = 1.0 / 0.9


def nt(a, b):
    return lax.dot_general(a, b, (((1,), (1,)), ((), ())), preferred_element_type=F32)


def tn(a, b):
    return lax.dot_general(a, b, (((0,), (0,)), ((), ())), preferred_element_type=F32)


def nn(a, b):
    return jnp.dot(a, b, preferred_element_type=F32)


SCRATCH = dict(
    x=((32, 8, D), BF),
    ks=((32, 8, D), jnp.int32),
    kt=((32, 8, D), jnp.int32),
    wqs=((3 * INNER, D), BF),
    wos=((INNER, D), BF),
    wqt=((3 * INNER, D), BF),
    wot=((INNER, D), BF),
    go=((NS, 8, D), BF),
    y_out=((NS, 8, D), BF),
    y_in=((NS, 8, D), BF),
    d_out=((NS, 8, D), BF),
    d_in=((NS, 8, D), BF),
    normed_s=((T, D), BF),
    normed_t=((T, D), BF),
    hs_s=((24, HD, T), BF),
    hs_t=((24, HD, T), BF),
    probs=((H, T, T), F32),
    mh_s=((H, HD, T), BF),
    mh_t=((H, HD, T), BF),
    mixed=((T, INNER), BF),
    dproj=((T, D), BF),
    dmh=((H, HD, T), BF),
    dh=((24, HD, T), BF),
    dqkv=((T, 3 * INNER), BF),
    dn=((T, D), F32),
    dsel=((2, 2, D, T), BF),
    dsel_in=((2, D, T), BF),
    perm=((D, D), BF),
    lt=((2, 2, D, T), BF),
    lt_in=((2, 2, D, T), BF),
    dx=((32, 8, D), BF),
)
SEMS = dict(
    load=(8,),
    store=(1,),
    a2a_s=(3, 31),
    a2a_r=(3, 31),
    core_s=(2, 4),
    core_r=(2, 4),
)
BATCHES = dict(time=(896, True), out=(384, False), space=(640, True))
for _n, (_w, _c) in BATCHES.items():
    SCRATCH.update({
        _n + "_g": ((8, 2, PB, _w), BF),
        _n + "_r1": ((2, 2, PB, _w), BF),
        _n + "_r2": ((2, 2, 2, PB, _w), BF),
    })
    SEMS.update({
        _n + "_r1_s": (2, 2), _n + "_r1_r": (2, 2), _n + "_r2_s": (2, 2, 2), _n + "_r2_r": (2, 2, 2),
    })
    if _c:
        SCRATCH.update({
            _n + "_c": ((2, 2, 4, 2, PB, 128), BF),
            _n + "_ci": ((3, 4, 2, PB, 128), BF),
            _n + "_cs": ((4, 4, RB, 128), BF),
            _n + "_cj": ((15, RB, 128), BF),
            _n + "_h": ((2, 4, RB, 896), BF),
            _n + "_r3": ((2, 3, RB, 896), BF),
            _n + "_z": ((2, 2, RB, 512), BF),
            _n + "_r4": ((3, RB, 512), BF),
        })
        SEMS.update({_n + "_r3_s": (2, 3), _n + "_r3_r": (2, 3), _n + "_r4_s": (3,), _n + "_r4_r": (3,)})
        SEMS.update({_n + "_ci_s": (3,), _n + "_ci_r": (3,), _n + "_cj_s": (15,), _n + "_cj_r": (15,)})


class Refs:
    pass


def body(*refs):
    ins, outs, rest = refs[:8], refs[8:13], refs[13:]
    m = Refs()
    for name, ref in zip(SCRATCH, rest[: len(SCRATCH)]):
        setattr(m, name, ref)
    for name, ref in zip(SEMS, rest[len(SCRATCH):]):
        setattr(m, name + "_sem", ref)
    dx_hbm, gqs, gos, gqt, got = outs

    dp = lax.axis_index("dp")
    me = lax.axis_index("seq")
    zh, core = dp // 2, lax.rem(dp, 2)
    cx, zl, cy = me // 8, lax.rem(me // 4, 2), lax.rem(me, 4)
    cz = zh * 2 + zl

    def place(x, y, z):
        return ((z // 2) * 2 + core, x * 8 + lax.rem(z, 2) * 4 + y)

    dests = (m.x, None, m.ks, m.kt, m.wqs, m.wos, m.wqt, m.wot)
    loads = [
        None if dst is None else pltpu.make_async_copy(src, dst, m.load_sem.at[i])
        for i, (src, dst) in enumerate(zip(ins, dests))
    ]
    loads[0].start()
    loads[4].start()

    barrier = pltpu.get_barrier_semaphore()

    def greet(d, carry):
        pl.semaphore_signal(
            barrier, inc=1, device_id=(dp, lax.rem(me + d, NS)), device_id_type=MESH
        )
        return carry

    lax.fori_loop(1, NS, greet, 0)
    other_core = (zh * 2 + 1 - core, me)
    pl.semaphore_signal(barrier, inc=1, device_id=other_core, device_id_type=MESH)
    far = (1 - zh) * 2 + core
    pl.semaphore_signal(barrier, inc=1, device_id=(far, me), device_id_type=MESH)
    pl.semaphore_signal(
        barrier, inc=1, device_id=(far, cx * 8 + (1 - zl) * 4 + cy), device_id_type=MESH
    )

    def a2a_copy(k, src, dst, d):
        to = lax.rem(me + d, NS)
        return pltpu.make_async_remote_copy(
            src_ref=src.at[to],
            dst_ref=dst.at[me],
            send_sem=m.a2a_s_sem.at[k, d - 1],
            recv_sem=m.a2a_r_sem.at[k, d - 1],
            device_id=(dp, to),
            device_id_type=MESH,
        )

    def a2a_start(k, src, dst):
        def step(d, carry):
            a2a_copy(k, src, dst, d).start()
            return carry

        lax.fori_loop(1, NS, step, 0)

    def a2a_send(k, src, dst, to):
        d = lax.rem(to - me + NS, NS)

        @pl.when(d != 0)
        def _():
            a2a_copy(k, src, dst, d).start()

    def a2a_wait(k, src, dst):
        def step(d, carry):
            frm = lax.rem(me + NS - d, NS)
            pltpu.make_async_remote_copy(
                src_ref=src.at[frm],
                dst_ref=dst.at[frm],
                send_sem=m.a2a_s_sem.at[k, d - 1],
                recv_sem=m.a2a_r_sem.at[k, d - 1],
                device_id=(dp, frm),
                device_id_type=MESH,
            ).wait_recv()
            return carry

        lax.fori_loop(1, NS, step, 0)

    def a2a_drain(k, src, dst):
        def step(d, carry):
            a2a_copy(k, src, dst, d).wait_send()
            return carry

        lax.fori_loop(1, NS, step, 0)

    def rows(fn, first=0, then=None):
        def step(i, carry):
            r = lax.rem(i + first, 8)
            fn(pl.ds(pl.multiple_of(r * 32, 32), 32), pl.ds(r * 4, 4))
            if then is not None:
                then(r)
            return carry

        lax.fori_loop(0, 8, step, 0)

    def flat(ref, blk):
        return ref[blk].astype(F32).reshape(32, D)

    def inv_of(zf):
        return lax.rsqrt(jnp.mean(zf * zf, axis=-1, keepdims=True) + 1e-06)

    def normalize(src, dst):
        def fn(r, blk):
            zf = flat(src, blk)
            dst[r, :] = (zf * inv_of(zf)).astype(BF)

        rows(fn)

    def heads(ref, js):
        return jnp.concatenate([ref[j].astype(F32) for j in js], axis=0)

    def qkv_heads(normed, w, hs):
        for n in range(3):
            part = nt(w[INNER * n: INNER * (n + 1), :], normed[...])
            hs[H * n: H * (n + 1)] = part.reshape(H, HD, T).astype(BF)

    def d_proj_mix(dy, keep, wo):
        def fn(r, blk):
            m.dproj[r, :] = (flat(dy, blk) * (flat(keep, blk) * KEEP)).astype(BF)

        rows(fn)
        m.dmh[...] = nt(wo[...], m.dproj[...]).reshape(H, HD, T).astype(BF)

    def some_heads(lo, hi, fn):
        def step(i, carry):
            for j in range(HEADS_AT_ONCE):
                fn(i * HEADS_AT_ONCE + j)
            return carry

        lax.fori_loop(lo // HEADS_AT_ONCE, hi // HEADS_AT_ONCE, step, 0)

    def softmax(q, k, mask):
        e = jnp.exp(tn(q, k) * SCALE)
        if mask is not None:
            e = jnp.where(mask, e, 0.0)
        return e * (1.0 / jnp.sum(e, axis=-1, keepdims=True))

    def attention_backward(h, p, p_low, q, k, v):
        dm = m.dmh[h]
        dp_ = tn(dm, v)
        ds = (p * (dp_ - jnp.sum(p * dp_, axis=-1, keepdims=True)) * SCALE).astype(BF)
        m.dh[h] = nt(k, ds).astype(BF)
        m.dh[h + 8] = nn(q, ds).astype(BF)
        m.dh[h + 16] = nn(dm, p_low).astype(BF)

    def gather_columns(sec):
        for c in range(2):
            z0 = heads(m.dh, [6 * c + i for i in range(6)])
            z1 = heads(m.dh, [12 + 6 * c + i for i in range(6)])
            parts = [z0[:128], z1[:128], z0[128:], z1[128:]]
            m.dsel[sec, c, 0:864] = jnp.concatenate(parts, axis=0).astype(BF)

    def gather_mixed(sec, mh):
        for c in range(2):
            hs = (2 * c, 2 * c + 1, 4 + 2 * c, 5 + 2 * c)
            m.dsel[sec, c, 864:1152] = heads(mh, hs).astype(BF)

    def input_backward(src, dy, dst, wq, then=None):
        m.dqkv[:, 0:1152] = heads(m.dh, range(16)).T.astype(BF)
        m.dqkv[:, 1152:1728] = heads(m.dh, range(16, 24)).T.astype(BF)
        for n in range(3):
            m.dn[:, 384 * n: 384 * (n + 1)] = nn(m.dqkv[...], wq[:, 384 * n: 384 * (n + 1)])

        def fn(r, blk):
            zf = flat(src, blk)
            inv = inv_of(zf)
            c = zf * inv
            dn = m.dn[r, :]
            dz = flat(dy, blk) + inv * (dn - c * jnp.mean(dn * c, axis=-1, keepdims=True))
            dst[blk] = dz.reshape(4, 8, D).astype(BF)

        rows(fn, me // 4, then)

    def core_copies(sec):
        pairs = (
            (m.lt.at[sec, 0], m.lt_in.at[sec, 0]),
            (m.lt.at[sec, 1], m.lt_in.at[sec, 1]),
            (m.dsel.at[sec, 1 - core, 0:864], m.dsel_in.at[sec, 0:864]),
            (m.dsel.at[sec, 1 - core, 864:1152], m.dsel_in.at[sec, 864:1152]),
        )
        return [
            pltpu.make_async_remote_copy(
                src_ref=src,
                dst_ref=dst,
                send_sem=m.core_s_sem.at[sec, i],
                recv_sem=m.core_r_sem.at[sec, i],
                device_id=other_core,
                device_id_type=MESH,
            )
            for i, (src, dst) in enumerate(pairs)
        ]

    def transpose_rows(sec, i, src):
        def step(n, carry):
            r = pl.ds(pl.multiple_of(n * 288, 288), 288)
            m.lt[sec, i, r, :] = nt(m.perm[r, :], src[...]).astype(BF)
            return carry

        lax.fori_loop(0, 4, step, 0)

    def grad_of(sec, i, o, lo, hi):
        r = slice(576 * o, 576 * (o + 1))
        acc = nt(m.lt[sec, i, r, :], m.dsel[sec, core, lo:hi, :])
        acc = acc + nt(m.lt_in[sec, i, r, :], m.dsel_in[sec, lo:hi, :])
        return acc

    def widen(acc, width):
        return jnp.concatenate([acc, jnp.zeros((acc.shape[0], width - acc.shape[1]), F32)], axis=1)

    def lower(acc):
        return jnp.concatenate([acc[36:72], jnp.zeros((4, acc.shape[1]), F32)], axis=0).astype(BF)

    def blocks(acc):
        return acc.reshape(4, 2, PB, acc.shape[1]).astype(BF)

    def grad_first(sec, n):
        dst = getattr(m, n + "_c")
        for o in range(2):
            acc = grad_of(sec, 0, o, 0, 256)
            dst[0, o] = blocks(acc[:, :128])
            dst[1, o] = blocks(acc[:, 128:])

    def grad_rest(sec, n):
        dst = getattr(m, n + "_g")
        for o in range(2):
            acc = grad_of(sec, 0, o, 256, 864)
            if n == "space":
                acc = widen(acc, 640)
            dst[4 * o: 4 * o + 4, :, :, 0: acc.shape[1]] = blocks(acc)

    def grad_out(sec, n):
        dst = getattr(m, n + "_g")
        for o in range(2):
            acc = grad_of(sec, 1, o, 864, 1152)
            if n == "out":
                dst[4 * o: 4 * o + 4] = blocks(widen(acc, 384))
            else:
                dst[4 * o: 4 * o + 4, :, :, 608:896] = blocks(acc)

    def ring(o):
        return cx if o == 0 else cy

    def on_first(o, i):
        return place(i, cy, cz) if o == 0 else place(cx, i, cz)

    def on_second(o, i):
        return place(cx, i, cz) if o == 0 else place(i, cy, cz)

    def remote(src, dst, ssem, rsem, to):
        return pltpu.make_async_remote_copy(
            src_ref=src, dst_ref=dst, send_sem=ssem, recv_sem=rsem, device_id=to, device_id_type=MESH
        )

    class Batch:
        def __init__(self, n):
            self.n = n
            for k in ("g", "r1", "r2", "h", "r3", "z", "r4", "c", "ci", "cs", "cj"):
                setattr(self, k, getattr(m, n + "_" + k, None))
            for k in ("r1", "r2", "r3", "r4", "ci", "cj"):
                for side in "sr":
                    name = k + "_" + side
                    setattr(self, name, getattr(m, n + "_" + name + "_sem", None))

        def first(self, o):
            i = ring(o)
            up, dn, opp = lax.rem(i + 1, 4), lax.rem(i + 3, 4), lax.rem(i + 2, 4)
            one = [
                remote(self.g.at[o * 4 + opp, k], self.r1.at[o, k],
                       self.r1_s.at[o, k], self.r1_r.at[o, k], on_first(o, to))
                for k, to in ((0, up), (1, dn))
            ]
            two = [
                [
                    remote(self.g.at[o * 4 + to, b], self.r2.at[o, k, b],
                           self.r2_s.at[o, k, b], self.r2_r.at[o, k, b], on_first(o, to))
                    for b in range(2)
                ]
                for k, to in ((0, up), (1, dn))
            ]
            return one, two, up, dn, i

        def start(self):
            firsts = [self.first(o) for o in range(2)]
            for one, two, up, dn, i in firsts:
                one[0].start()
                one[1].start()
            for one, two, up, dn, i in firsts:
                two[0][1].start()
                two[1][0].start()

        def relay(self):
            for o in range(2):
                one, two, up, dn, i = self.first(o)
                for side, chunk, b in ((0, up, 0), (1, dn, 1)):
                    one[side].wait_recv()
                    acc = self.g[o * 4 + chunk, b].astype(F32)
                    acc = acc + self.r1[o, side].astype(F32)
                    self.g[o * 4 + chunk, b] = acc.astype(BF)
                    two[side][b].start()

        def second_copies(self, o):
            j = ring(1 - o)
            return [
                remote(self.h.at[o, lax.rem(j + d, 4)], self.r3.at[o, d - 1],
                       self.r3_s.at[o, d - 1], self.r3_r.at[o, d - 1],
                       on_second(o, lax.rem(j + d, 4)))
                for d in (1, 2, 3)
            ]

        def arrived(self, o):
            one, two, up, dn, i = self.first(o)
            for side in two:
                for c in side:
                    c.wait_recv()

        def total(self, o, e):
            acc = self.g[o * 4 + ring(o), e].astype(F32)
            acc = acc + self.r2[o, 0, e].astype(F32)
            return acc + self.r2[o, 1, e].astype(F32)

        def second(self):
            for o in range(2):
                self.arrived(o)
                if self.n == "space":
                    b_out.arrived(o)
                for e in range(2):
                    acc = self.total(o, e)
                    if self.n == "space":
                        acc = jnp.concatenate([acc[:, :608], b_out.total(o, e)[:, :288]], axis=1)
                    self.h[o, 2 * e] = acc[0:40].astype(BF)
                    self.h[o, 2 * e + 1] = lower(acc)
                for c in self.second_copies(o):
                    c.start()

        def z_copies(self):
            copies = []
            for d in (1, 2, 3):
                z = lax.rem(cz + d, 4)
                copies.append(
                    remote(self.z.at[lax.rem(z, 2), z // 2], self.r4.at[d - 1],
                           self.r4_s.at[d - 1], self.r4_r.at[d - 1], place(cx, cy, z))
                )
            return copies

        def third(self):
            for o in range(2):
                for c in self.second_copies(o):
                    c.wait_recv()
                acc = self.h[o, ring(1 - o)].astype(F32)
                for d in range(3):
                    acc = acc + self.r3[o, d].astype(F32)
                for z in range(2):
                    low = 608 + 144 * z
                    v = jnp.concatenate(
                        [acc[:, 304 * z: 304 * (z + 1)], acc[:, low: low + 144]], axis=1
                    )
                    self.z[o, z] = widen(v, 512).astype(BF)
            for c in self.z_copies():
                c.start()

        def ci_copies(self):
            copies = []
            for d in (1, 2, 3):
                z = lax.rem(cz + d, 4)
                copies.append(
                    remote(self.c.at[z // 2, lax.rem(z, 2)], self.ci.at[d - 1],
                           self.ci_s.at[d - 1], self.ci_r.at[d - 1], place(cx, cy, z))
                )
            return copies

        def cj_copies(self):
            copies = []
            for d in range(1, 16):
                x, y = lax.rem(cx + d // 4, 4), lax.rem(cy + d % 4, 4)
                a, b = x * (1 - zl) + y * zl, y * (1 - zl) + x * zl
                copies.append(
                    remote(self.cs.at[a, b], self.cj.at[d - 1],
                           self.cj_s.at[d - 1], self.cj_r.at[d - 1], place(x, y, cz))
                )
            return copies

        def c_start(self):
            for c in self.ci_copies():
                c.start()

        def c_second(self):
            for c in self.ci_copies():
                c.wait_recv()

            def add(a, carry):
                for e in range(2):
                    acc = self.c[zh, zl, a, e].astype(F32)
                    for d in range(3):
                        acc = acc + self.ci[d, a, e].astype(F32)
                    self.cs[a, 2 * e] = acc[0:40].astype(BF)
                    self.cs[a, 2 * e + 1] = lower(acc)
                return carry

            lax.fori_loop(0, 4, add, 0)
            for c in self.cj_copies():
                c.start()

        def c_end(self):
            for c in self.cj_copies():
                c.wait_recv()
            a, b = cx * (1 - zl) + cy * zl, cy * (1 - zl) + cx * zl
            acc = self.cs[a, b].astype(F32)
            for d in range(15):
                acc = acc + self.cj[d].astype(F32)
            return acc

        def end(self):
            for c in self.z_copies():
                c.wait_recv()
            acc = self.z[zl, zh].astype(F32)
            for d in range(3):
                acc = acc + self.r4[d].astype(F32)
            return acc

        def drain(self):
            for o in range(2):
                one, two, up, dn, i = self.first(o)
                for c in one + two[0] + two[1]:
                    c.wait_send()
            if self.c is not None:
                for c in self.second_copies(0) + self.second_copies(1) + self.z_copies():
                    c.wait_send()
                for c in self.ci_copies() + self.cj_copies():
                    c.wait_send()

    b_time, b_out, b_space = Batch("time"), Batch("out"), Batch("space")

    loads[0].wait()
    normalize(m.x, m.normed_s)
    pl.semaphore_wait(barrier, NS + 2)
    a2a_start(0, ins[1], m.go)
    own = pltpu.make_async_copy(ins[1].at[me], m.go.at[me], m.load_sem.at[1])
    own.start()
    loads[4].wait()
    for i in (5, 2, 7, 3, 6):
        loads[i].start()
    qkv_heads(m.normed_s, m.wqs, m.hs_s)

    loads[2].wait()
    loads[5].wait()
    for half in range(2):
        q_part, f_part = slice(128 * half, 128 * (half + 1)), slice(16 * half, 16 * (half + 1))

        def spatial_head(h):
            p = softmax(m.hs_s[h, :, q_part], m.hs_s[h + 8], None)
            m.probs[h, q_part, :] = p
            m.mh_s[h, :, q_part] = nt(m.hs_s[h + 16], p.astype(BF)).astype(BF)

        some_heads(0, H, spatial_head)
        part = jnp.concatenate([m.mh_s[h, :, q_part].astype(F32) for h in range(H)], axis=0)
        m.mixed[q_part, :] = part.T.astype(BF)
        for n in range(3):
            c = slice(384 * n, 384 * (n + 1))
            proj = nn(m.mixed[q_part, :], m.wos[:, c]).reshape(16, 8, 384)
            keep = m.ks[f_part, :, c].astype(F32) * KEEP
            m.y_out[f_part, :, c] = (m.x[f_part, :, c].astype(F32) + proj * keep).astype(BF)

        def send_part(i, carry):
            a2a_send(1, m.y_out, m.y_in, 16 * half + lax.rem(me + i, 16))
            return carry

        lax.fori_loop(0, 16, send_part, 0)
    m.y_in[me] = m.y_out[me]

    def perm_step(n, carry):
        o, a = n // 4, lax.rem(n, 4)
        row = lax.broadcasted_iota(jnp.int32, (PB, D), 0)
        col = lax.broadcasted_iota(jnp.int32, (PB, D), 1)
        pairs = []
        for b in (0, 2):
            s0 = (a * (1 - o) + b * o) * 8 + o * 4 + b * (1 - o) + a * o
            s1 = s0 + 8 * o + 1 - o
            target = jnp.where(row < 36, row + 36 * s0, row + 36 * s1 - 36)
            pairs.append(jnp.where(col == target, 1.0, 0.0))
        both = jnp.concatenate(pairs, axis=0).astype(BF)
        m.perm[pl.ds(pl.multiple_of(n * 144, 144), 144), :] = both
        return carry

    lax.fori_loop(0, 8, perm_step, 0)
    gather_mixed(1, m.mh_s)
    core_copies(1)[3].start()

    own.wait()
    a2a_wait(0, m.go, m.go)
    loads[3].wait()
    loads[7].wait()
    d_proj_mix(m.go, m.kt, m.wot)
    transpose_rows(0, 1, m.dproj)
    core_copies(0)[1].start()
    transpose_rows(1, 0, m.normed_s)
    core_copies(1)[0].start()
    a2a_wait(1, m.y_out, m.y_in)
    normalize(m.y_in, m.normed_t)
    loads[6].wait()
    qkv_heads(m.normed_t, m.wqt, m.hs_t)

    def temporal_head(h):
        i = lax.broadcasted_iota(jnp.int32, (T, T), 0)
        j = lax.broadcasted_iota(jnp.int32, (T, T), 1)
        mask = ((i - j) & 7) == 0
        q, k, v = m.hs_t[h], m.hs_t[h + 8], m.hs_t[h + 16]
        p = softmax(q, k, mask)
        p_low = p.astype(BF)
        m.mh_t[h] = nt(v, p_low).astype(BF)
        attention_backward(h, p, p_low, q, k, v)

    some_heads(0, H, temporal_head)
    def send_rows(r):
        for j in range(4):
            a2a_send(2, m.d_out, m.d_in, r * 4 + lax.rem(me + j, 4))

    input_backward(m.y_in, m.go, m.d_out, m.wqt, send_rows)
    m.d_in[me] = m.d_out[me]
    gather_columns(0)
    gather_mixed(0, m.mh_t)
    core_copies(0)[2].start()
    core_copies(0)[3].start()
    transpose_rows(0, 0, m.normed_t)
    core_copies(0)[0].start()
    for c in core_copies(0):
        c.wait_recv()
    grad_rest(0, "time")
    grad_out(0, "time")
    b_time.start()
    grad_first(0, "time")
    b_time.c_start()

    a2a_wait(2, m.d_out, m.d_in)
    d_proj_mix(m.d_in, m.ks, m.wos)
    transpose_rows(1, 1, m.dproj)
    core_copies(1)[1].start()

    def spatial_back(h):
        p = m.probs[h]
        attention_backward(h, p, p.astype(BF), m.hs_s[h], m.hs_s[h + 8], m.hs_s[h + 16])

    some_heads(0, H // 2, spatial_back)
    b_time.relay()
    core_copies(1)[1].wait_recv()
    core_copies(1)[3].wait_recv()
    grad_out(1, "out")
    b_out.start()
    some_heads(H // 2, H, spatial_back)
    gather_columns(1)
    core_copies(1)[2].start()
    b_time.second()
    b_time.c_second()
    core_copies(1)[0].wait_recv()
    core_copies(1)[2].wait_recv()
    grad_rest(1, "space")
    b_space.start()
    grad_first(1, "space")
    b_space.c_start()
    b_out.relay()
    b_time.third()
    input_backward(m.x, m.d_in, m.dx, m.wqs)
    store = pltpu.make_async_copy(m.dx, dx_hbm, m.store_sem.at[0])
    store.start()
    b_space.relay()
    first = b_time.c_end()
    rest = b_time.end()
    gqt[...] = jnp.concatenate([first[0:36], rest[0:36, 0:304]], axis=1)
    got[...] = rest[0:36, 304:448]
    b_space.second()
    b_space.c_second()
    b_space.third()
    first = b_space.c_end()
    rest = b_space.end()
    gqs[...] = jnp.concatenate([first[0:36], rest[0:36, 0:304]], axis=1)
    gos[...] = rest[0:36, 304:448]

    a2a_drain(0, ins[1], m.go)
    a2a_drain(1, m.y_out, m.y_in)
    a2a_drain(2, m.d_out, m.d_in)
    for c in core_copies(0) + core_copies(1):
        c.wait_send()
    b_time.drain()
    b_out.drain()
    b_space.drain()
    store.wait()


def hand_over(*refs):
    sem = refs[10]
    copies = [pltpu.make_async_copy(refs[i], refs[5 + i], sem.at[i]) for i in range(5)]
    for c in copies:
        c.start()
    for c in copies:
        c.wait()


def shards(
    block_input,
    out_grad,
    spatial_keep,
    temporal_keep,
    spatial_qkv,
    spatial_out,
    temporal_qkv,
    temporal_out,
):
    hbm = pl.BlockSpec(memory_space=pl.ANY)
    vmem = pl.BlockSpec(memory_space=pltpu.VMEM)
    outs = pl.pallas_call(
        body,
        out_shape=(
            jax.ShapeDtypeStruct((32, 8, D), BF),
            jax.ShapeDtypeStruct((36, 432), F32),
            jax.ShapeDtypeStruct((36, 144), F32),
            jax.ShapeDtypeStruct((36, 432), F32),
            jax.ShapeDtypeStruct((36, 144), F32),
        ),
        in_specs=[hbm] * 8,
        out_specs=(hbm, vmem, vmem, vmem, vmem),
        scratch_shapes=[pltpu.VMEM(s, d) for s, d in SCRATCH.values()]
        + [pltpu.SemaphoreType.DMA(s) for s in SEMS.values()],
        compiler_params=pltpu.CompilerParams(
            collective_id=0, has_side_effects=True, vmem_limit_bytes=63 * 2**20
        ),
    )(
        block_input.reshape(32, 8, D),
        out_grad.reshape(32, 8, D),
        spatial_keep.reshape(32, 8, D),
        temporal_keep.reshape(32, 8, D),
        spatial_qkv.T,
        spatial_out.T,
        temporal_qkv.T,
        temporal_out.T,
    )
    outs = pl.pallas_call(
        hand_over,
        out_shape=tuple(jax.ShapeDtypeStruct(o.shape, o.dtype) for o in outs),
        in_specs=[vmem] * 5,
        out_specs=(hbm,) * 5,
        scratch_shapes=[pltpu.SemaphoreType.DMA((5,))],
    )(*outs)
    return (outs[0].reshape(1, 1, T, D),) + tuple(outs[1:])


def solution(mesh):
    return jax.shard_map(
        shards,
        mesh=mesh,
        in_specs=(
            P("dp", "seq", None, None),
            P("dp", "seq", None, None),
            P("dp", "seq", None, None),
            P("dp", None, "seq", None),
            P(),
            P(),
            P(),
            P(),
        ),
        out_specs=(
            P("dp", "seq", None, None),
            P("seq", "dp"),
            P("seq", "dp"),
            P("seq", "dp"),
            P("seq", "dp"),
        ),
        check_vma=False,
    )
```

```python
import jax
import jax.numpy as jnp
from jax import lax
from jax.experimental import pallas as pl
from jax.experimental.pallas import tpu as pltpu
from jax.sharding import PartitionSpec as P

D = 1152
H = 8
HD = 72
INNER = 576
T = 256
NS = 32
RB = 40
PB = 72
HEADS_AT_ONCE = 4
MESH = pl.DeviceIdType.MESH
BF = jnp.bfloat16
F32 = jnp.float32
SCALE = HD ** (-0.5)
KEEP = 1.0 / 0.9


def nt(a, b):
    return lax.dot_general(a, b, (((1,), (1,)), ((), ())), preferred_element_type=F32)


def tn(a, b):
    return lax.dot_general(a, b, (((0,), (0,)), ((), ())), preferred_element_type=F32)


def nn(a, b):
    return jnp.dot(a, b, preferred_element_type=F32)


SCRATCH = dict(
    x=((32, 8, D), BF),
    ks=((32, 8, D), jnp.int32),
    kt=((32, 8, D), jnp.int32),
    wqs=((3 * INNER, D), BF),
    wos=((INNER, D), BF),
    wqt=((3 * INNER, D), BF),
    wot=((INNER, D), BF),
    go=((NS, 8, D), BF),
    y_out=((NS, 8, D), BF),
    y_in=((NS, 8, D), BF),
    d_out=((NS, 8, D), BF),
    d_in=((NS, 8, D), BF),
    normed_s=((T, D), BF),
    normed_t=((T, D), BF),
    hs_s=((24, HD, T), BF),
    hs_t=((24, HD, T), BF),
    probs=((H, T, T), F32),
    mh_s=((H, HD, T), BF),
    mh_t=((H, HD, T), BF),
    mixed=((T, INNER), BF),
    dproj=((T, D), BF),
    dmh=((H, HD, T), BF),
    dh=((24, HD, T), BF),
    dqkv=((T, 3 * INNER), BF),
    dn=((T, D), F32),
    dsel=((2, 2, D, T), BF),
    dsel_in=((2, D, T), BF),
    perm=((D, D), BF),
    lt=((2, 2, D, T), BF),
    lt_in=((2, 2, D, T), BF),
    dx=((32, 8, D), BF),
)
SEMS = dict(
    load=(8,),
    store=(1,),
    a2a_s=(3, 31),
    a2a_r=(3, 31),
    core_s=(2, 4),
    core_r=(2, 4),
)
BATCHES = dict(time=(896, True), out=(384, False), space=(640, True))
for _n, (_w, _c) in BATCHES.items():
    SCRATCH.update({
        _n + "_g": ((8, 2, PB, _w), BF),
        _n + "_r1": ((2, 2, PB, _w), BF),
        _n + "_r2": ((2, 2, 2, PB, _w), BF),
    })
    SEMS.update({
        _n + "_r1_s": (2, 2), _n + "_r1_r": (2, 2), _n + "_r2_s": (2, 2, 2), _n + "_r2_r": (2, 2, 2),
    })
    if _c:
        SCRATCH.update({
            _n + "_c": ((2, 2, 4, 2, PB, 128), BF),
            _n + "_ci": ((3, 4, 2, PB, 128), BF),
            _n + "_cs": ((4, 4, RB, 128), BF),
            _n + "_cj": ((15, RB, 128), BF),
            _n + "_h": ((2, 4, RB, 896), BF),
            _n + "_r3": ((2, 3, RB, 896), BF),
            _n + "_z": ((2, 2, RB, 512), BF),
            _n + "_r4": ((3, RB, 512), BF),
        })
        SEMS.update({_n + "_r3_s": (2, 3), _n + "_r3_r": (2, 3), _n + "_r4_s": (3,), _n + "_r4_r": (3,)})
        SEMS.update({_n + "_ci_s": (3,), _n + "_ci_r": (3,), _n + "_cj_s": (15,), _n + "_cj_r": (15,)})


class Refs:
    pass


def body(*refs):
    ins, outs, rest = refs[:8], refs[8:13], refs[13:]
    m = Refs()
    for name, ref in zip(SCRATCH, rest[: len(SCRATCH)]):
        setattr(m, name, ref)
    for name, ref in zip(SEMS, rest[len(SCRATCH):]):
        setattr(m, name + "_sem", ref)
    dx_hbm, gqs, gos, gqt, got = outs

    dp = lax.axis_index("dp")
    me = lax.axis_index("seq")
    zh, core = dp // 2, lax.rem(dp, 2)
    cx, zl, cy = me // 8, lax.rem(me // 4, 2), lax.rem(me, 4)
    cz = zh * 2 + zl

    def place(x, y, z):
        return ((z // 2) * 2 + core, x * 8 + lax.rem(z, 2) * 4 + y)

    dests = (m.x, None, m.ks, m.kt, m.wqs, m.wos, m.wqt, m.wot)
    loads = [
        None if dst is None else pltpu.make_async_copy(src, dst, m.load_sem.at[i])
        for i, (src, dst) in enumerate(zip(ins, dests))
    ]
    loads[0].start()
    loads[4].start()

    barrier = pltpu.get_barrier_semaphore()

    def greet(d, carry):
        pl.semaphore_signal(
            barrier, inc=1, device_id=(dp, lax.rem(me + d, NS)), device_id_type=MESH
        )
        return carry

    lax.fori_loop(1, NS, greet, 0)
    other_core = (zh * 2 + 1 - core, me)
    pl.semaphore_signal(barrier, inc=1, device_id=other_core, device_id_type=MESH)
    far = (1 - zh) * 2 + core
    pl.semaphore_signal(barrier, inc=1, device_id=(far, me), device_id_type=MESH)
    pl.semaphore_signal(
        barrier, inc=1, device_id=(far, cx * 8 + (1 - zl) * 4 + cy), device_id_type=MESH
    )

    def a2a_copy(k, src, dst, d):
        to = lax.rem(me + d, NS)
        return pltpu.make_async_remote_copy(
            src_ref=src.at[to],
            dst_ref=dst.at[me],
            send_sem=m.a2a_s_sem.at[k, d - 1],
            recv_sem=m.a2a_r_sem.at[k, d - 1],
            device_id=(dp, to),
            device_id_type=MESH,
        )

    def a2a_start(k, src, dst):
        def step(d, carry):
            a2a_copy(k, src, dst, d).start()
            return carry

        lax.fori_loop(1, NS, step, 0)

    def a2a_send(k, src, dst, to):
        d = lax.rem(to - me + NS, NS)

        @pl.when(d != 0)
        def _():
            a2a_copy(k, src, dst, d).start()

    def a2a_wait(k, src, dst):
        def step(d, carry):
            frm = lax.rem(me + NS - d, NS)
            pltpu.make_async_remote_copy(
                src_ref=src.at[frm],
                dst_ref=dst.at[frm],
                send_sem=m.a2a_s_sem.at[k, d - 1],
                recv_sem=m.a2a_r_sem.at[k, d - 1],
                device_id=(dp, frm),
                device_id_type=MESH,
            ).wait_recv()
            return carry

        lax.fori_loop(1, NS, step, 0)

    def a2a_drain(k, src, dst):
        def step(d, carry):
            a2a_copy(k, src, dst, d).wait_send()
            return carry

        lax.fori_loop(1, NS, step, 0)

    def rows(fn, first=0, then=None):
        def step(i, carry):
            r = lax.rem(i + first, 8)
            fn(pl.ds(pl.multiple_of(r * 32, 32), 32), pl.ds(r * 4, 4))
            if then is not None:
                then(r)
            return carry

        lax.fori_loop(0, 8, step, 0)

    def flat(ref, blk):
        return ref[blk].astype(F32).reshape(32, D)

    def inv_of(zf):
        return lax.rsqrt(jnp.mean(zf * zf, axis=-1, keepdims=True) + 1e-06)

    def normalize(src, dst):
        def fn(r, blk):
            zf = flat(src, blk)
            dst[r, :] = (zf * inv_of(zf)).astype(BF)

        rows(fn)

    def heads(ref, js):
        return jnp.concatenate([ref[j].astype(F32) for j in js], axis=0)

    def qkv_heads(normed, w, hs):
        for n in range(3):
            part = nt(w[INNER * n: INNER * (n + 1), :], normed[...])
            hs[H * n: H * (n + 1)] = part.reshape(H, HD, T).astype(BF)

    def d_proj_mix(dy, keep, wo):
        def fn(r, blk):
            m.dproj[r, :] = (flat(dy, blk) * (flat(keep, blk) * KEEP)).astype(BF)

        rows(fn)
        m.dmh[...] = nt(wo[...], m.dproj[...]).reshape(H, HD, T).astype(BF)

    def some_heads(lo, hi, fn):
        def step(i, carry):
            for j in range(HEADS_AT_ONCE):
                fn(i * HEADS_AT_ONCE + j)
            return carry

        lax.fori_loop(lo // HEADS_AT_ONCE, hi // HEADS_AT_ONCE, step, 0)

    def softmax(q, k, mask):
        e = jnp.exp(tn(q, k) * SCALE)
        if mask is not None:
            e = jnp.where(mask, e, 0.0)
        return e * (1.0 / jnp.sum(e, axis=-1, keepdims=True))

    def attention_backward(h, p, p_low, q, k, v):
        dm = m.dmh[h]
        dp_ = tn(dm, v)
        ds = (p * (dp_ - jnp.sum(p * dp_, axis=-1, keepdims=True)) * SCALE).astype(BF)
        m.dh[h] = nt(k, ds).astype(BF)
        m.dh[h + 8] = nn(q, ds).astype(BF)
        m.dh[h + 16] = nn(dm, p_low).astype(BF)

    def gather_columns(sec):
        for c in range(2):
            z0 = heads(m.dh, [6 * c + i for i in range(6)])
            z1 = heads(m.dh, [12 + 6 * c + i for i in range(6)])
            parts = [z0[:128], z1[:128], z0[128:], z1[128:]]
            m.dsel[sec, c, 0:864] = jnp.concatenate(parts, axis=0).astype(BF)

    def gather_mixed(sec, mh):
        for c in range(2):
            hs = (2 * c, 2 * c + 1, 4 + 2 * c, 5 + 2 * c)
            m.dsel[sec, c, 864:1152] = heads(mh, hs).astype(BF)

    def input_backward(src, dy, dst, wq, then=None, between=None):
        m.dqkv[:, 0:1152] = heads(m.dh, range(16)).T.astype(BF)
        m.dqkv[:, 1152:1728] = heads(m.dh, range(16, 24)).T.astype(BF)
        for n in range(3):
            m.dn[:, 384 * n: 384 * (n + 1)] = nn(m.dqkv[...], wq[:, 384 * n: 384 * (n + 1)])

        if between is not None:
            between()

        def fn(r, blk):
            zf = flat(src, blk)
            inv = inv_of(zf)
            c = zf * inv
            dn = m.dn[r, :]
            dz = flat(dy, blk) + inv * (dn - c * jnp.mean(dn * c, axis=-1, keepdims=True))
            dst[blk] = dz.reshape(4, 8, D).astype(BF)

        rows(fn, me // 4, then)

    def core_copies(sec):
        pairs = (
            (m.lt.at[sec, 0], m.lt_in.at[sec, 0]),
            (m.lt.at[sec, 1], m.lt_in.at[sec, 1]),
            (m.dsel.at[sec, 1 - core, 0:864], m.dsel_in.at[sec, 0:864]),
            (m.dsel.at[sec, 1 - core, 864:1152], m.dsel_in.at[sec, 864:1152]),
        )
        return [
            pltpu.make_async_remote_copy(
                src_ref=src,
                dst_ref=dst,
                send_sem=m.core_s_sem.at[sec, i],
                recv_sem=m.core_r_sem.at[sec, i],
                device_id=other_core,
                device_id_type=MESH,
            )
            for i, (src, dst) in enumerate(pairs)
        ]

    def transpose_rows(sec, i, src):
        def step(n, carry):
            r = pl.ds(pl.multiple_of(n * 288, 288), 288)
            m.lt[sec, i, r, :] = nt(m.perm[r, :], src[...]).astype(BF)
            return carry

        lax.fori_loop(0, 4, step, 0)

    def grad_of(sec, i, o, lo, hi):
        r = slice(576 * o, 576 * (o + 1))
        acc = nt(m.lt[sec, i, r, :], m.dsel[sec, core, lo:hi, :])
        acc = acc + nt(m.lt_in[sec, i, r, :], m.dsel_in[sec, lo:hi, :])
        return acc

    def widen(acc, width):
        return jnp.concatenate([acc, jnp.zeros((acc.shape[0], width - acc.shape[1]), F32)], axis=1)

    def lower(acc):
        return jnp.concatenate([acc[36:72], jnp.zeros((4, acc.shape[1]), F32)], axis=0).astype(BF)

    def blocks(acc):
        return acc.reshape(4, 2, PB, acc.shape[1]).astype(BF)

    def grad_first(sec, n):
        dst = getattr(m, n + "_c")
        for o in range(2):
            acc = grad_of(sec, 0, o, 0, 256)
            dst[0, o] = blocks(acc[:, :128])
            dst[1, o] = blocks(acc[:, 128:])

    def grad_rest(sec, n):
        dst = getattr(m, n + "_g")
        for o in range(2):
            acc = grad_of(sec, 0, o, 256, 864)
            if n == "space":
                acc = widen(acc, 640)
            dst[4 * o: 4 * o + 4, :, :, 0: acc.shape[1]] = blocks(acc)

    def grad_out(sec, n):
        dst = getattr(m, n + "_g")
        for o in range(2):
            acc = grad_of(sec, 1, o, 864, 1152)
            if n == "out":
                dst[4 * o: 4 * o + 4] = blocks(widen(acc, 384))
            else:
                dst[4 * o: 4 * o + 4, :, :, 608:896] = blocks(acc)

    def ring(o):
        return cx if o == 0 else cy

    def on_first(o, i):
        return place(i, cy, cz) if o == 0 else place(cx, i, cz)

    def on_second(o, i):
        return place(cx, i, cz) if o == 0 else place(i, cy, cz)

    def remote(src, dst, ssem, rsem, to):
        return pltpu.make_async_remote_copy(
            src_ref=src, dst_ref=dst, send_sem=ssem, recv_sem=rsem, device_id=to, device_id_type=MESH
        )

    class Batch:
        def __init__(self, n):
            self.n = n
            for k in ("g", "r1", "r2", "h", "r3", "z", "r4", "c", "ci", "cs", "cj"):
                setattr(self, k, getattr(m, n + "_" + k, None))
            for k in ("r1", "r2", "r3", "r4", "ci", "cj"):
                for side in "sr":
                    name = k + "_" + side
                    setattr(self, name, getattr(m, n + "_" + name + "_sem", None))

        def first(self, o):
            i = ring(o)
            up, dn, opp = lax.rem(i + 1, 4), lax.rem(i + 3, 4), lax.rem(i + 2, 4)
            one = [
                remote(self.g.at[o * 4 + opp, k], self.r1.at[o, k],
                       self.r1_s.at[o, k], self.r1_r.at[o, k], on_first(o, to))
                for k, to in ((0, up), (1, dn))
            ]
            two = [
                [
                    remote(self.g.at[o * 4 + to, b], self.r2.at[o, k, b],
                           self.r2_s.at[o, k, b], self.r2_r.at[o, k, b], on_first(o, to))
                    for b in range(2)
                ]
                for k, to in ((0, up), (1, dn))
            ]
            return one, two, up, dn, i

        def start(self):
            firsts = [self.first(o) for o in range(2)]
            for one, two, up, dn, i in firsts:
                one[0].start()
                one[1].start()
            for one, two, up, dn, i in firsts:
                two[0][1].start()
                two[1][0].start()

        def relay(self):
            for o in range(2):
                one, two, up, dn, i = self.first(o)
                for side, chunk, b in ((0, up, 0), (1, dn, 1)):
                    one[side].wait_recv()
                    acc = self.g[o * 4 + chunk, b].astype(F32)
                    acc = acc + self.r1[o, side].astype(F32)
                    self.g[o * 4 + chunk, b] = acc.astype(BF)
                    two[side][b].start()

        def second_copies(self, o):
            j = ring(1 - o)
            return [
                remote(self.h.at[o, lax.rem(j + d, 4)], self.r3.at[o, d - 1],
                       self.r3_s.at[o, d - 1], self.r3_r.at[o, d - 1],
                       on_second(o, lax.rem(j + d, 4)))
                for d in (1, 2, 3)
            ]

        def arrived(self, o):
            one, two, up, dn, i = self.first(o)
            for side in two:
                for c in side:
                    c.wait_recv()

        def total(self, o, e):
            acc = self.g[o * 4 + ring(o), e].astype(F32)
            acc = acc + self.r2[o, 0, e].astype(F32)
            return acc + self.r2[o, 1, e].astype(F32)

        def second(self):
            for o in range(2):
                self.arrived(o)
                if self.n == "space":
                    b_out.arrived(o)
                for e in range(2):
                    acc = self.total(o, e)
                    if self.n == "space":
                        acc = jnp.concatenate([acc[:, :608], b_out.total(o, e)[:, :288]], axis=1)
                    self.h[o, 2 * e] = acc[0:40].astype(BF)
                    self.h[o, 2 * e + 1] = lower(acc)
                for c in self.second_copies(o):
                    c.start()

        def z_copies(self):
            copies = []
            for d in (1, 2, 3):
                z = lax.rem(cz + d, 4)
                copies.append(
                    remote(self.z.at[lax.rem(z, 2), z // 2], self.r4.at[d - 1],
                           self.r4_s.at[d - 1], self.r4_r.at[d - 1], place(cx, cy, z))
                )
            return copies

        def third(self):
            for o in range(2):
                for c in self.second_copies(o):
                    c.wait_recv()
                acc = self.h[o, ring(1 - o)].astype(F32)
                for d in range(3):
                    acc = acc + self.r3[o, d].astype(F32)
                for z in range(2):
                    low = 608 + 144 * z
                    v = jnp.concatenate(
                        [acc[:, 304 * z: 304 * (z + 1)], acc[:, low: low + 144]], axis=1
                    )
                    self.z[o, z] = widen(v, 512).astype(BF)
            for c in self.z_copies():
                c.start()

        def ci_copies(self):
            copies = []
            for d in (1, 2, 3):
                z = lax.rem(cz + d, 4)
                copies.append(
                    remote(self.c.at[z // 2, lax.rem(z, 2)], self.ci.at[d - 1],
                           self.ci_s.at[d - 1], self.ci_r.at[d - 1], place(cx, cy, z))
                )
            return copies

        def cj_copies(self):
            copies = []
            for d in range(1, 16):
                x, y = lax.rem(cx + d // 4, 4), lax.rem(cy + d % 4, 4)
                a, b = x * (1 - zl) + y * zl, y * (1 - zl) + x * zl
                copies.append(
                    remote(self.cs.at[a, b], self.cj.at[d - 1],
                           self.cj_s.at[d - 1], self.cj_r.at[d - 1], place(x, y, cz))
                )
            return copies

        def c_start(self):
            for c in self.ci_copies():
                c.start()

        def c_second(self):
            for c in self.ci_copies():
                c.wait_recv()

            def add(a, carry):
                for e in range(2):
                    acc = self.c[zh, zl, a, e].astype(F32)
                    for d in range(3):
                        acc = acc + self.ci[d, a, e].astype(F32)
                    self.cs[a, 2 * e] = acc[0:40].astype(BF)
                    self.cs[a, 2 * e + 1] = lower(acc)
                return carry

            lax.fori_loop(0, 4, add, 0)
            for c in self.cj_copies():
                c.start()

        def c_end(self):
            for c in self.cj_copies():
                c.wait_recv()
            a, b = cx * (1 - zl) + cy * zl, cy * (1 - zl) + cx * zl
            acc = self.cs[a, b].astype(F32)
            for d in range(15):
                acc = acc + self.cj[d].astype(F32)
            return acc

        def end(self):
            for c in self.z_copies():
                c.wait_recv()
            acc = self.z[zl, zh].astype(F32)
            for d in range(3):
                acc = acc + self.r4[d].astype(F32)
            return acc

        def drain(self):
            for o in range(2):
                one, two, up, dn, i = self.first(o)
                for c in one + two[0] + two[1]:
                    c.wait_send()
            if self.c is not None:
                for c in self.second_copies(0) + self.second_copies(1) + self.z_copies():
                    c.wait_send()
                for c in self.ci_copies() + self.cj_copies():
                    c.wait_send()

    b_time, b_out, b_space = Batch("time"), Batch("out"), Batch("space")

    loads[0].wait()
    normalize(m.x, m.normed_s)
    pl.semaphore_wait(barrier, NS + 2)
    a2a_start(0, ins[1], m.go)
    own = pltpu.make_async_copy(ins[1].at[me], m.go.at[me], m.load_sem.at[1])
    own.start()
    loads[4].wait()
    for i in (5, 2, 7, 3, 6):
        loads[i].start()
    qkv_heads(m.normed_s, m.wqs, m.hs_s)

    loads[2].wait()
    loads[5].wait()
    for half in range(2):
        q_part, f_part = slice(128 * half, 128 * (half + 1)), slice(16 * half, 16 * (half + 1))

        def spatial_head(h):
            p = softmax(m.hs_s[h, :, q_part], m.hs_s[h + 8], None)
            m.probs[h, q_part, :] = p
            m.mh_s[h, :, q_part] = nt(m.hs_s[h + 16], p.astype(BF)).astype(BF)

        some_heads(0, H, spatial_head)
        part = jnp.concatenate([m.mh_s[h, :, q_part].astype(F32) for h in range(H)], axis=0)
        m.mixed[q_part, :] = part.T.astype(BF)
        for n in range(3):
            c = slice(384 * n, 384 * (n + 1))
            proj = nn(m.mixed[q_part, :], m.wos[:, c]).reshape(16, 8, 384)
            keep = m.ks[f_part, :, c].astype(F32) * KEEP
            m.y_out[f_part, :, c] = (m.x[f_part, :, c].astype(F32) + proj * keep).astype(BF)

        def send_part(i, carry):
            a2a_send(1, m.y_out, m.y_in, 16 * half + lax.rem(me + i, 16))
            return carry

        lax.fori_loop(0, 16, send_part, 0)
    m.y_in[me] = m.y_out[me]

    def perm_step(n, carry):
        o, a = n // 4, lax.rem(n, 4)
        row = lax.broadcasted_iota(jnp.int32, (PB, D), 0)
        col = lax.broadcasted_iota(jnp.int32, (PB, D), 1)
        pairs = []
        for b in (0, 2):
            s0 = (a * (1 - o) + b * o) * 8 + o * 4 + b * (1 - o) + a * o
            s1 = s0 + 8 * o + 1 - o
            target = jnp.where(row < 36, row + 36 * s0, row + 36 * s1 - 36)
            pairs.append(jnp.where(col == target, 1.0, 0.0))
        both = jnp.concatenate(pairs, axis=0).astype(BF)
        m.perm[pl.ds(pl.multiple_of(n * 144, 144), 144), :] = both
        return carry

    lax.fori_loop(0, 8, perm_step, 0)
    gather_mixed(1, m.mh_s)
    core_copies(1)[3].start()

    own.wait()
    a2a_wait(0, m.go, m.go)
    loads[3].wait()
    loads[7].wait()
    d_proj_mix(m.go, m.kt, m.wot)
    transpose_rows(0, 1, m.dproj)
    core_copies(0)[1].start()
    transpose_rows(1, 0, m.normed_s)
    core_copies(1)[0].start()
    a2a_wait(1, m.y_out, m.y_in)
    normalize(m.y_in, m.normed_t)
    loads[6].wait()
    qkv_heads(m.normed_t, m.wqt, m.hs_t)

    def temporal_head(h):
        i = lax.broadcasted_iota(jnp.int32, (T, T), 0)
        j = lax.broadcasted_iota(jnp.int32, (T, T), 1)
        mask = ((i - j) & 7) == 0
        q, k, v = m.hs_t[h], m.hs_t[h + 8], m.hs_t[h + 16]
        p = softmax(q, k, mask)
        p_low = p.astype(BF)
        m.mh_t[h] = nt(v, p_low).astype(BF)
        attention_backward(h, p, p_low, q, k, v)

    some_heads(0, H, temporal_head)
    def send_rows(r):
        for j in range(4):
            a2a_send(2, m.d_out, m.d_in, r * 4 + lax.rem(me + j, 4))

    input_backward(m.y_in, m.go, m.d_out, m.wqt, send_rows)
    m.d_in[me] = m.d_out[me]
    gather_columns(0)
    gather_mixed(0, m.mh_t)
    core_copies(0)[2].start()
    core_copies(0)[3].start()
    transpose_rows(0, 0, m.normed_t)
    core_copies(0)[0].start()
    for c in core_copies(0):
        c.wait_recv()
    grad_rest(0, "time")
    grad_out(0, "time")
    b_time.start()
    grad_first(0, "time")
    b_time.c_start()

    a2a_wait(2, m.d_out, m.d_in)
    d_proj_mix(m.d_in, m.ks, m.wos)
    transpose_rows(1, 1, m.dproj)
    core_copies(1)[1].start()

    def spatial_back(h):
        p = m.probs[h]
        attention_backward(h, p, p.astype(BF), m.hs_s[h], m.hs_s[h + 8], m.hs_s[h + 16])

    some_heads(0, H // 2, spatial_back)
    b_time.relay()
    core_copies(1)[1].wait_recv()
    core_copies(1)[3].wait_recv()
    grad_out(1, "out")
    b_out.start()
    some_heads(H // 2, H, spatial_back)
    gather_columns(1)
    core_copies(1)[2].start()
    b_time.second()
    b_time.c_second()
    core_copies(1)[0].wait_recv()
    core_copies(1)[2].wait_recv()
    grad_rest(1, "space")
    b_space.start()
    grad_first(1, "space")
    b_space.c_start()
    b_out.relay()
    b_time.third()
    input_backward(m.x, m.d_in, m.dx, m.wqs, between=b_space.relay)
    store = pltpu.make_async_copy(m.dx, dx_hbm, m.store_sem.at[0])
    store.start()
    first = b_time.c_end()
    rest = b_time.end()
    gqt[...] = jnp.concatenate([first[0:36], rest[0:36, 0:304]], axis=1)
    got[...] = rest[0:36, 304:448]
    b_space.second()
    b_space.c_second()
    b_space.third()
    first = b_space.c_end()
    rest = b_space.end()
    gqs[...] = jnp.concatenate([first[0:36], rest[0:36, 0:304]], axis=1)
    gos[...] = rest[0:36, 304:448]

    a2a_drain(0, ins[1], m.go)
    a2a_drain(1, m.y_out, m.y_in)
    a2a_drain(2, m.d_out, m.d_in)
    for c in core_copies(0) + core_copies(1):
        c.wait_send()
    b_time.drain()
    b_out.drain()
    b_space.drain()
    store.wait()


def hand_over(*refs):
    sem = refs[10]
    copies = [pltpu.make_async_copy(refs[i], refs[5 + i], sem.at[i]) for i in range(5)]
    for c in copies:
        c.start()
    for c in copies:
        c.wait()


def shards(
    block_input,
    out_grad,
    spatial_keep,
    temporal_keep,
    spatial_qkv,
    spatial_out,
    temporal_qkv,
    temporal_out,
):
    hbm = pl.BlockSpec(memory_space=pl.ANY)
    vmem = pl.BlockSpec(memory_space=pltpu.VMEM)
    outs = pl.pallas_call(
        body,
        out_shape=(
            jax.ShapeDtypeStruct((32, 8, D), BF),
            jax.ShapeDtypeStruct((36, 432), F32),
            jax.ShapeDtypeStruct((36, 144), F32),
            jax.ShapeDtypeStruct((36, 432), F32),
            jax.ShapeDtypeStruct((36, 144), F32),
        ),
        in_specs=[hbm] * 8,
        out_specs=(hbm, vmem, vmem, vmem, vmem),
        scratch_shapes=[pltpu.VMEM(s, d) for s, d in SCRATCH.values()]
        + [pltpu.SemaphoreType.DMA(s) for s in SEMS.values()],
        compiler_params=pltpu.CompilerParams(
            collective_id=0, has_side_effects=True, vmem_limit_bytes=63 * 2**20
        ),
    )(
        block_input.reshape(32, 8, D),
        out_grad.reshape(32, 8, D),
        spatial_keep.reshape(32, 8, D),
        temporal_keep.reshape(32, 8, D),
        spatial_qkv.T,
        spatial_out.T,
        temporal_qkv.T,
        temporal_out.T,
    )
    outs = pl.pallas_call(
        hand_over,
        out_shape=tuple(jax.ShapeDtypeStruct(o.shape, o.dtype) for o in outs),
        in_specs=[vmem] * 5,
        out_specs=(hbm,) * 5,
        scratch_shapes=[pltpu.SemaphoreType.DMA((5,))],
    )(*outs)
    return (outs[0].reshape(1, 1, T, D),) + tuple(outs[1:])


def solution(mesh):
    return jax.shard_map(
        shards,
        mesh=mesh,
        in_specs=(
            P("dp", "seq", None, None),
            P("dp", "seq", None, None),
            P("dp", "seq", None, None),
            P("dp", None, "seq", None),
            P(),
            P(),
            P(),
            P(),
        ),
        out_specs=(
            P("dp", "seq", None, None),
            P("seq", "dp"),
            P("seq", "dp"),
            P("seq", "dp"),
            P("seq", "dp"),
        ),
        check_vma=False,
    )
```
